1024 devices in a mesh: ctx: 64 (over y, z_lo, core), ch: 16 (over x, z_hi).
Axes of the slice: x: 4, y: 8, z: 16 (z_hi: 4, z_lo: 4; z = z_hi * 4 + z_lo), core: 2. Of those that a mesh axis runs over, the one named last changes fastest.
Arguments:
- gate_input: bfloat16 [1024, 8192], P('ch', 'ctx'), may hold values from -6 to 6
- key_input: bfloat16 [1024, 8192], P('ch', 'ctx'), may hold values from -6 to 6
- value_input: bfloat16 [1024, 8192], P('ch', 'ctx'), may hold values from -6 to 6
- features: float32 [64, 8192], P('ch', 'ctx'), may hold values from -6 to 6
- filter_weight: float32 [64, 1024], P(None, 'ch'), may hold values from -0.75 to 0.75
- out_grad: bfloat16 [1024, 8192], P('ch', 'ctx'), may hold values from -6 to 6
Outputs:
- output: bfloat16 [1024, 8192], P('ch', 'ctx')
- gate_grad: bfloat16 [1024, 8192], P('ch', 'ctx')
- key_grad: bfloat16 [1024, 8192], P('ch', 'ctx')
- value_grad: bfloat16 [1024, 8192], P('ch', 'ctx')
- weight_grad: float32 [64, 1024], P(None, 'ch')
The draws below stay inside these ranges and needn't reach their ends.
All inputs are finite; a program needn't handle non-finite values.
Results may differ from the reference program's by a relative error of at most 0.0019.
Values sent between devices are 32-bit elements; how exact they have to be, the bound alone decides.
A program may use at most 32 MiB of HBM per device.

```python
import math
import jax
import jax.numpy as jnp
from jax import lax

CHANNELS = 1024
FEAT = 64
TOKENS = 8192


def level_of(stream_key, dims, split, least, largest):
    factor_of = 1.0
    for position, blocks in split:
        steps = jax.random.uniform(jax.random.fold_in(jax.random.fold_in(stream_key, 6), position), (blocks,), jnp.float32, least / len(split), largest / len(split))
        factor_of = factor_of * jnp.repeat(jnp.exp(steps), dims[position] // blocks).reshape((-1,) + (1,) * (len(dims) - 1 - position))
    return factor_of


def scatter_about(own_key, shape, deviation, limit, split=(), dtype=jnp.bfloat16):
    drawn = jax.random.normal(own_key, shape, jnp.float32) * deviation
    if len(split) > 0:
        drawn = level_of(own_key, shape, split, -0.22, 0.18) * drawn
    return jnp.clip(drawn, min=-limit, max=limit).astype(dtype)


def setup_inputs(seed: int = 0) -> dict:
    key_list = jax.random.split(jax.random.key(seed), 7)
    return {
        "gate_input": scatter_about(key_list[0], (CHANNELS, TOKENS), 1.0, 6.0, ((0, 16), (1, 64))),
        "key_input": scatter_about(key_list[1], (CHANNELS, TOKENS), 1.0, 6.0, ((0, 16), (1, 64))),
        "value_input": scatter_about(key_list[2], (CHANNELS, TOKENS), 1.0, 6.0, ((0, 16), (1, 64))),
        "features": scatter_about(key_list[3], (FEAT, TOKENS), 1.0, 6.0, ((0, 16), (1, 64)), jnp.float32),
        "filter_weight": scatter_about(key_list[4], (FEAT, CHANNELS), FEAT ** -0.5, 0.75, ((1, 16),), jnp.float32),
        "out_grad": scatter_about(key_list[5], (CHANNELS, TOKENS), 1.0, 6.0, ((0, 16), (1, 64))),
    }


def spectrum(signal, padded):
    return jnp.fft.rfft(signal, n=padded, axis=0)

def back_time(product, padded, keep_len):
    return jnp.fft.irfft(product, n=padded, axis=0)[:keep_len]

def reference(gate_input, key_input, value_input, features, filter_weight, out_grad):
    seq_len = TOKENS
    padded = 2 * seq_len
    scaling = 1.0 / math.sqrt(seq_len)
    gate_vals = gate_input.T.astype(jnp.float32)
    key_vals = key_input.T.astype(jnp.float32)
    value_vals = value_input.T.astype(jnp.float32)
    upstream = out_grad.T.astype(jnp.float32)
    feats = features.T
    mixed_in = key_vals * value_vals
    filters = jnp.dot(feats, filter_weight, precision=lax.Precision.HIGHEST) * scaling
    mixed_spec = spectrum(mixed_in, padded)
    filter_spec = spectrum(filters, padded)
    conv_out = back_time(mixed_spec * filter_spec, padded, seq_len)
    output = (gate_vals * conv_out).astype(jnp.bfloat16)
    gate_grad = (upstream * conv_out).astype(jnp.bfloat16)
    inner_term = upstream * gate_vals
    inner_spec = spectrum(inner_term, padded)
    mixed_grad = back_time(inner_spec * jnp.conj(filter_spec), padded, seq_len)
    key_grad = (mixed_grad * value_vals).astype(jnp.bfloat16)
    value_grad = (mixed_grad * key_vals).astype(jnp.bfloat16)
    taps_grad = back_time(inner_spec * jnp.conj(mixed_spec), padded, seq_len)
    weight_grad = jnp.dot(feats.T, taps_grad, precision=lax.Precision.HIGHEST) * (scaling * scaling)
    return (output.T, gate_grad.T, key_grad.T, value_grad.T, weight_grad)
```

```python
import functools
import math

import jax
import jax.numpy as jnp
import numpy as np
from jax import lax
from jax.experimental import pallas as pl
from jax.experimental.pallas import tpu as pltpu
from jax.sharding import PartitionSpec as P

MESH = pl.DeviceIdType.MESH
HIGHEST = lax.Precision.HIGHEST
f32 = jnp.float32
bf16 = jnp.bfloat16
LANES = 128


def make_tables(shards):
    outer = 2 * shards
    padded = outer * LANES
    rows = -(-(shards + 1) // 8) * 8
    r = np.arange(rows)
    live = (r <= shards).astype(np.float64)
    natural = np.arange(shards)
    by_parity = np.concatenate([natural[0::2], natural[1::2]])

    def angles(left, right, period):
        return 2.0 * np.pi * ((left[:, None] * right[None, :]) % period) / period

    first, last = [], []
    weight = np.where((r == 0) | (r == shards), 1.0, 2.0) * live / padded
    for order in (natural, by_parity):
        turn = angles(r, order, outer)
        table = np.concatenate([np.cos(turn), np.sin(turn)], axis=0) * np.tile(live, 2)[:, None]
        first.append(table)
        turn = angles(order, r, outer)
        table = np.concatenate([np.cos(turn) * weight, -np.sin(turn) * weight], axis=1)
        last.append(table)
    q = np.arange(LANES)
    turn = angles(q, q, LANES)
    cos, sin = np.cos(turn), np.sin(turn)
    forward = np.block([[cos, -sin], [sin, cos]])
    backward = np.block([[cos, sin], [-sin, cos]])
    turn = angles(r, q, padded)
    twist = [np.cos(turn), np.sin(turn)]
    return tuple(np.stack(table).astype(np.float32) for table in (first, last, [forward, backward], twist))


def halves(x):
    high = x.astype(bf16)
    return high, (x - high.astype(f32)).astype(bf16)


def dot(a, b):
    return jnp.dot(a, b, preferred_element_type=f32)


def dot_t(a, b):
    return lax.dot_general(a, b, (((1,), (1,)), ((), ())), precision=HIGHEST, preferred_element_type=f32)


def spectra(signals, first, mid, cos, sin):
    rows = cos.shape[0]
    high, low = halves(jnp.concatenate(signals, axis=1))
    outer = dot(first, jnp.concatenate([high, low, high], axis=0))
    turned = []
    for index in range(len(signals)):
        part = outer[:, index * LANES : (index + 1) * LANES]
        along, across = part[:rows], part[rows:]
        turned.append(
            jnp.concatenate([along * cos - across * sin, -(across * cos + along * sin)], axis=1)
        )
    high, low = halves(jnp.concatenate(turned, axis=0))
    return dot(high, mid[0]) + dot(low, mid[0]) + dot(high, mid[1])


def signals_of(products, last, mid, cos, sin):
    rows = cos.shape[0]
    high, low = halves(jnp.concatenate(products, axis=0))
    inner = dot(high, mid[0]) + dot(low, mid[0]) + dot(high, mid[1])
    turned = []
    for index in range(len(products)):
        part = inner[index * rows : (index + 1) * rows]
        real, imag = part[:, :LANES], part[:, LANES:]
        turned.append(jnp.concatenate([real * cos - imag * sin, imag * cos + real * sin], axis=0))
    high, low = halves(jnp.concatenate(turned, axis=1))
    return dot(last[0], high) + dot(last[0], low) + dot(last[1], high)


def times(a, b):
    ar, ai, br, bi = a[:, :LANES], a[:, LANES:], b[:, :LANES], b[:, LANES:]
    return jnp.concatenate([ar * br - ai * bi, ar * bi + ai * br], axis=1)


def times_conj(a, b):
    ar, ai, br, bi = a[:, :LANES], a[:, LANES:], b[:, :LANES], b[:, LANES:]
    return jnp.concatenate([ar * br + ai * bi, ai * br - ar * bi], axis=1)


def kernel(
    shards,
    groups,
    gate_in,
    key_in,
    value_in,
    feats_in,
    weight_in,
    upstream_in,
    first_in,
    last_in,
    mid_in,
    twist_in,
    output,
    gate_grad,
    key_grad,
    value_grad,
    weight_grad,
    gate,
    key,
    value,
    upstream,
    weight,
    first,
    last,
    mid,
    twist,
    first_split,
    last_split,
    mid_split,
    feats,
    send_sig,
    recv_sig,
    send_filt,
    recv_filt,
    send_taps,
    recv_taps,
    send_part,
    recv_part,
    send_sum,
    recv_sum,
    send_out,
    recv_out,
    in_sems,
    table_sems,
    own_sem,
    send_sems,
    recv_sems,
):
    me = lax.axis_index("ctx")
    group = lax.axis_index("ch")
    owners = shards // 2
    chip = me // 2
    core = me % 2
    scaling = 1.0 / math.sqrt(shards * LANES)

    inputs = [
        pltpu.make_async_copy(src, dst, in_sems.at[n])
        for n, (src, dst) in enumerate(
            [(key_in, key), (value_in, value), (upstream_in, upstream), (gate_in, gate), (weight_in, weight)]
        )
    ]
    tables = [
        pltpu.make_async_copy(src, dst, table_sems.at[n])
        for n, (src, dst) in enumerate([(first_in, first), (mid_in, mid), (twist_in, twist), (last_in, last)])
    ]

    def push(src, dst, phase, where):
        pltpu.make_async_remote_copy(
            src_ref=src,
            dst_ref=dst,
            send_sem=send_sems.at[phase],
            recv_sem=recv_sems.at[phase],
            device_id=where,
            device_id_type=MESH,
        ).start()

    def loop(low, high, step):
        def body(k, carry):
            step(k)
            return carry

        lax.fori_loop(low, high, body, 0)

    def arrived(ref, count, phase):
        part = ref.at[pl.ds(0, count)]
        pltpu.make_async_copy(part, part, recv_sems.at[phase]).wait()

    def sent(ref, count, phase):
        part = ref.at[pl.ds(0, count)]
        pltpu.make_async_copy(part, part, send_sems.at[phase]).wait()

    for copy in inputs:
        copy.start()

    barrier = pltpu.get_barrier_semaphore()

    @pl.when(core == 1)
    def _():
        def tell(k):
            pl.semaphore_signal(barrier, inc=1, device_id={"ctx": me ^ k, "ch": group}, device_id_type=MESH)

        def tell_groups(k):
            other = group ^ k
            pl.semaphore_signal(barrier, inc=1, device_id={"ctx": me, "ch": other}, device_id_type=MESH)
            pl.semaphore_signal(barrier, inc=1, device_id={"ctx": me - 1, "ch": other}, device_id_type=MESH)

        loop(1, groups, tell_groups)
        loop(1, shards, tell)
        for copy in tables:
            copy.start()
        pl.semaphore_wait(barrier, owners - 1 + groups - 1)

    @pl.when(core == 0)
    def _():
        pl.semaphore_wait(barrier, owners + groups - 1)

    def push_feats(k):
        push(feats_in, feats.at[core * groups + group], 0, {"ctx": 2 * chip + 1, "ch": group ^ k})

    loop(1, groups, push_feats)
    own_feats = pltpu.make_async_copy(feats_in, feats.at[core * groups + group], own_sem)

    @pl.when(core == 0)
    def _():
        push_feats(0)

    @pl.when(core == 1)
    def _():
        own_feats.start()

    for copy in inputs[:4]:
        copy.wait()
    key_vals, value_vals = key[...].astype(f32), value[...].astype(f32)
    gate_vals, up_vals = gate[...].astype(f32), upstream[...].astype(f32)
    mixed, inner = key_vals * value_vals, up_vals * gate_vals
    send_sig[:, 0, :] = mixed[:owners]
    send_sig[:, 1, :] = mixed[owners:]
    send_sig[:, 2, :] = inner[:owners]
    send_sig[:, 3, :] = inner[owners:]

    def push_sig(k):
        to = chip ^ k
        push(send_sig.at[to], recv_sig.at[me], 1, {"ctx": 2 * to + 1, "ch": group})

    loop(1, owners, push_sig)

    @pl.when(core == 0)
    def _():
        push_sig(0)

    inputs[4].wait()

    @pl.when(core == 1)
    def _():
        recv_sig[pl.ds(me, 1)] = send_sig[pl.ds(chip, 1)]
        eye = (
            lax.broadcasted_iota(jnp.int32, (2 * owners, 2 * owners), 0)
            == lax.broadcasted_iota(jnp.int32, (2 * owners, 2 * owners), 1)
        ).astype(f32)
        weight_t = dot_t(eye, weight[...])
        for copy in tables:
            copy.wait()
        cos, sin = twist[0], twist[1]
        rows = cos.shape[0]
        for n in range(2):
            high, low = halves(first[n])
            first_split[n] = jnp.concatenate([high, high, low], axis=1)
            last_split[2 * n], last_split[2 * n + 1] = halves(last[n])
            mid_split[2 * n], mid_split[2 * n + 1] = halves(mid[n])
        forward, backward = (mid_split[0], mid_split[1]), (mid_split[2], mid_split[3])
        lasts = [(last_split[0], last_split[1]), (last_split[2], last_split[3])]

        own_feats.wait()
        arrived(feats, 2 * groups - 1, 0)
        per = feats.shape[1]
        feats_all = jnp.concatenate(
            [
                feats[:groups].reshape(groups * per, LANES),
                feats[groups:].reshape(groups * per, LANES),
            ],
            axis=1,
        )
        filt = jnp.dot(weight_t, feats_all, precision=HIGHEST, preferred_element_type=f32) * scaling
        send_filt[:, 0, :] = filt[:owners, :LANES]
        send_filt[:, 1, :] = filt[:owners, LANES:]
        send_filt[:, 2, :] = filt[owners:, :LANES]
        send_filt[:, 3, :] = filt[owners:, LANES:]

        def push_filt(k):
            to = chip ^ k
            push(send_filt.at[to], recv_filt.at[chip], 2, {"ctx": 2 * to + 1, "ch": group})

        loop(1, owners, push_filt)
        recv_filt[pl.ds(chip, 1)] = send_filt[pl.ds(chip, 1)]

        arrived(recv_sig, shards - 1, 1)
        specs = spectra([recv_sig[:, n, :] for n in range(4)], first_split[0], forward, cos, sin)
        mixed_specs = [specs[:rows], specs[rows : 2 * rows]]
        inner_specs = [specs[2 * rows : 3 * rows], specs[3 * rows :]]
        taps = signals_of(
            [times_conj(inner_specs[n], mixed_specs[n]) for n in range(2)], lasts[1], backward, cos, sin
        )
        send_taps[:, 0, :] = taps[:owners, :LANES]
        send_taps[:, 1, :] = taps[owners:, :LANES]
        send_taps[:, 2, :] = taps[:owners, LANES:]
        send_taps[:, 3, :] = taps[owners:, LANES:]

        def push_taps(k):
            to = chip ^ k
            push(send_taps.at[to], recv_taps.at[chip], 3, {"ctx": 2 * to + 1, "ch": group})

        loop(1, owners, push_taps)
        recv_taps[pl.ds(chip, 1)] = send_taps[pl.ds(chip, 1)]

        arrived(recv_filt, owners - 1, 2)
        filt_specs = spectra(
            [
                jnp.concatenate([recv_filt[:, 2 * n, :], recv_filt[:, 2 * n + 1, :]], axis=0)
                for n in range(2)
            ],
            first_split[1],
            forward,
            cos,
            sin,
        )
        filt_specs = [filt_specs[:rows], filt_specs[rows:]]
        results = signals_of(
            [times(mixed_specs[n], filt_specs[n]) for n in range(2)]
            + [times_conj(inner_specs[n], filt_specs[n]) for n in range(2)],
            lasts[0],
            backward,
            cos,
            sin,
        )
        for n in range(4):
            send_out[:, n, :] = results[:, n * LANES : (n + 1) * LANES]

        def push_out(k):
            to = me ^ k
            push(send_out.at[to], recv_out.at[chip], 4, {"ctx": to, "ch": group})

        loop(1, shards, push_out)
        recv_out[pl.ds(chip, 1)] = send_out[pl.ds(me, 1)]

        arrived(recv_taps, owners - 1, 3)
        taps_here = jnp.concatenate(
            [
                jnp.concatenate([recv_taps[:, 0, :], recv_taps[:, 1, :]], axis=1),
                jnp.concatenate([recv_taps[:, 2, :], recv_taps[:, 3, :]], axis=1),
            ],
            axis=0,
        )
        part = dot_t(taps_here, feats_all)
        send_part[:, 0, :] = jnp.concatenate([part[:owners], part[owners:]], axis=1)

        def push_part(k):
            to = chip ^ k
            push(send_part.at[to], recv_part.at[chip], 5, {"ctx": 2 * to + 1, "ch": group})

        loop(1, owners, push_part)
        recv_part[pl.ds(chip, 1)] = send_part[pl.ds(chip, 1)]

        arrived(recv_part, owners - 1, 5)
        send_sum[pl.ds(0, 1)] = jnp.sum(recv_part[...], axis=0, keepdims=True) * (scaling * scaling)

        def push_sum(k):
            push(send_sum.at[0], recv_sum.at[chip], 6, {"ctx": me ^ k, "ch": group})

        loop(1, shards, push_sum)
        recv_sum[pl.ds(chip, 1)] = send_sum[pl.ds(0, 1)]
        arrived(recv_out, owners - 1, 4)
        sent(send_filt, owners - 1, 2)
        sent(send_taps, owners - 1, 3)
        sent(send_out, shards - 1, 4)
        sent(send_part, owners - 1, 5)
        sent(feats, groups - 1, 0)
        sent(send_sig, owners - 1, 1)

    @pl.when(core == 0)
    def _():
        arrived(recv_out, owners, 4)
        sent(feats, groups, 0)
        sent(send_sig, owners, 1)

    conv = jnp.concatenate([recv_out[:, 0, :], recv_out[:, 1, :]], axis=0)
    mixed_grad = jnp.concatenate([recv_out[:, 2, :], recv_out[:, 3, :]], axis=0)
    output[...] = (gate[...].astype(f32) * conv).astype(bf16)
    gate_grad[...] = (upstream[...].astype(f32) * conv).astype(bf16)
    key_grad[...] = (mixed_grad * value[...].astype(f32)).astype(bf16)
    value_grad[...] = (mixed_grad * key[...].astype(f32)).astype(bf16)

    @pl.when(core == 1)
    def _():
        arrived(recv_sum, owners - 1, 6)
        sent(send_sum, shards - 1, 6)

    @pl.when(core == 0)
    def _():
        arrived(recv_sum, owners, 6)

    total = recv_sum[:, 0, :]
    half = total.shape[1] // 2
    grad_rows = jnp.concatenate([total[:, :half], total[:, half:]], axis=0)
    eye = (
        lax.broadcasted_iota(jnp.int32, (half, half), 0) == lax.broadcasted_iota(jnp.int32, (half, half), 1)
    ).astype(f32)
    weight_grad[...] = dot_t(eye, grad_rows)


def on_device(gate_input, key_input, value_input, features, filter_weight, out_grad):
    shards, groups = lax.axis_size("ctx"), lax.axis_size("ch")
    channels, length = gate_input.shape
    feat = filter_weight.shape[0]
    owners = shards // 2
    assert channels == 2 * owners and length == LANES and feat == LANES // 2
    tables = make_tables(shards)
    hbm = pl.BlockSpec(memory_space=pl.ANY)
    vmem = pl.BlockSpec(memory_space=pltpu.VMEM)
    rows = lambda count, width: pltpu.VMEM((count, width, LANES), f32)
    block = jax.ShapeDtypeStruct((channels, length), bf16)
    per = features.shape[0]
    return pl.pallas_call(
        functools.partial(kernel, shards, groups),
        out_shape=(block, block, block, block, jax.ShapeDtypeStruct((feat, channels), f32)),
        in_specs=[hbm] * 10,
        out_specs=(vmem,) * 5,
        scratch_shapes=[
            *[pltpu.VMEM((channels, length), bf16)] * 4,
            pltpu.VMEM(filter_weight.shape, f32),
            *[pltpu.VMEM(table.shape, f32) for table in tables],
            pltpu.VMEM((2, tables[0].shape[1], 3 * tables[0].shape[2]), bf16),
            pltpu.VMEM((4, *tables[1].shape[1:]), bf16),
            pltpu.VMEM((4, *tables[2].shape[1:]), bf16),
            rows(2 * groups, per),
            rows(owners, 4),
            rows(shards, 4),
            rows(owners, 4),
            rows(owners, 4),
            rows(owners, 4),
            rows(owners, 4),
            rows(owners, 1),
            rows(owners, 1),
            rows(shards, 1),
            rows(owners, 1),
            rows(shards, 4),
            rows(owners, 4),
            pltpu.SemaphoreType.DMA((5,)),
            pltpu.SemaphoreType.DMA((4,)),
            pltpu.SemaphoreType.DMA,
            pltpu.SemaphoreType.DMA((7,)),
            pltpu.SemaphoreType.DMA((7,)),
        ],
        compiler_params=pltpu.CompilerParams(
            collective_id=0, has_side_effects=True, vmem_limit_bytes=56 * 1024 * 1024
        ),
    )(gate_input, key_input, value_input, features, filter_weight, out_grad, *tables)


def solution(mesh):
    placed = (
        P("ch", "ctx"),
        P("ch", "ctx"),
        P("ch", "ctx"),
        P("ch", "ctx"),
        P(None, "ch"),
        P("ch", "ctx"),
    )
    return jax.shard_map(
        on_device,
        mesh=mesh,
        in_specs=placed,
        out_specs=(P("ch", "ctx"), P("ch", "ctx"), P("ch", "ctx"), P("ch", "ctx"), P(None, "ch")),
        check_vma=False,
    )
```

```python
import functools
import math

import jax
import jax.numpy as jnp
import numpy as np
from jax import lax
from jax.experimental import pallas as pl
from jax.experimental.pallas import tpu as pltpu
from jax.sharding import PartitionSpec as P

MESH = pl.DeviceIdType.MESH
HIGHEST = lax.Precision.HIGHEST
f32 = jnp.float32
bf16 = jnp.bfloat16
LANES = 128


def make_tables(shards):
    outer = 2 * shards
    padded = outer * LANES
    rows = -(-(shards + 1) // 8) * 8
    r = np.arange(rows)
    live = (r <= shards).astype(np.float64)
    natural = np.arange(shards)
    by_parity = np.concatenate([natural[0::2], natural[1::2]])

    def angles(left, right, period):
        return 2.0 * np.pi * ((left[:, None] * right[None, :]) % period) / period

    first, last = [], []
    weight = np.where((r == 0) | (r == shards), 1.0, 2.0) * live / padded
    for order in (natural, by_parity):
        turn = angles(r, order, outer)
        table = np.concatenate([np.cos(turn), np.sin(turn)], axis=0) * np.tile(live, 2)[:, None]
        first.append(table)
        turn = angles(order, r, outer)
        table = np.concatenate([np.cos(turn) * weight, -np.sin(turn) * weight], axis=1)
        last.append(table)
    q = np.arange(LANES)
    turn = angles(q, q, LANES)
    cos, sin = np.cos(turn), np.sin(turn)
    forward = np.block([[cos, -sin], [sin, cos]])
    backward = np.block([[cos, sin], [-sin, cos]])
    turn = angles(r, q, padded)
    twist = [np.cos(turn), np.sin(turn)]
    return tuple(np.stack(table).astype(np.float32) for table in (first, last, [forward, backward], twist))


def halves(x):
    high = x.astype(bf16)
    return high, (x - high.astype(f32)).astype(bf16)


def dot(a, b):
    return jnp.dot(a, b, preferred_element_type=f32)


def dot_t(a, b):
    return lax.dot_general(a, b, (((1,), (1,)), ((), ())), precision=HIGHEST, preferred_element_type=f32)


def spectra(signals, first, mid, cos, sin):
    rows = cos.shape[0]
    high, low = halves(jnp.concatenate(signals, axis=1))
    outer = dot(first, jnp.concatenate([high, low, high], axis=0))
    turned = []
    for index in range(len(signals)):
        part = outer[:, index * LANES : (index + 1) * LANES]
        along, across = part[:rows], part[rows:]
        turned.append(
            jnp.concatenate([along * cos - across * sin, -(across * cos + along * sin)], axis=1)
        )
    high, low = halves(jnp.concatenate(turned, axis=0))
    return dot(high, mid[0]) + dot(low, mid[0]) + dot(high, mid[1])


def signals_of(products, last, mid, cos, sin):
    rows = cos.shape[0]
    high, low = halves(jnp.concatenate(products, axis=0))
    inner = dot(high, mid[0]) + dot(low, mid[0]) + dot(high, mid[1])
    turned = []
    for index in range(len(products)):
        part = inner[index * rows : (index + 1) * rows]
        real, imag = part[:, :LANES], part[:, LANES:]
        turned.append(jnp.concatenate([real * cos - imag * sin, imag * cos + real * sin], axis=0))
    high, low = halves(jnp.concatenate(turned, axis=1))
    return dot(last[0], high) + dot(last[0], low) + dot(last[1], high)


def times(a, b):
    ar, ai, br, bi = a[:, :LANES], a[:, LANES:], b[:, :LANES], b[:, LANES:]
    return jnp.concatenate([ar * br - ai * bi, ar * bi + ai * br], axis=1)


def times_conj(a, b):
    ar, ai, br, bi = a[:, :LANES], a[:, LANES:], b[:, :LANES], b[:, LANES:]
    return jnp.concatenate([ar * br + ai * bi, ai * br - ar * bi], axis=1)


def kernel(
    shards,
    groups,
    gate_in,
    key_in,
    value_in,
    feats_in,
    weight_in,
    upstream_in,
    first_in,
    last_in,
    mid_in,
    twist_in,
    recv_out,
    recv_sum,
    gate,
    key,
    value,
    upstream,
    weight,
    first,
    last,
    mid,
    twist,
    first_split,
    last_split,
    mid_split,
    feats,
    send_sig,
    recv_sig,
    send_filt,
    recv_filt,
    send_taps,
    recv_taps,
    send_part,
    recv_part,
    send_sum,
    send_out,
    in_sems,
    table_sems,
    own_sem,
    feat_sems,
    feat_sent,
    send_sems,
    recv_sems,
    hello,
    ready,
    all_in,
):
    me = lax.axis_index("ctx")
    group = lax.axis_index("ch")
    owners = shards // 2
    chip = me // 2
    core = me % 2
    scaling = 1.0 / math.sqrt(shards * LANES)
    deep = 4 if groups % 4 == 0 else 1
    wide = groups // deep
    rank = (group % deep) * wide + group // deep
    kind = jnp.minimum(group % deep, 2)
    known = wide * jnp.minimum(kind + 1, 2)
    settled = jnp.minimum(wide * (kind + 1), groups)
    greeters = known - jnp.where(kind < 2, 1, 0)
    hub = 1
    at_hub = chip == hub

    def ranked(r):
        return (r % wide) * deep + r // wide

    inputs = [
        pltpu.make_async_copy(src, dst, in_sems.at[n])
        for n, (src, dst) in enumerate(
            [(key_in, key), (value_in, value), (upstream_in, upstream), (gate_in, gate), (weight_in, weight)]
        )
    ]
    tables = [
        pltpu.make_async_copy(src, dst, table_sems.at[n])
        for n, (src, dst) in enumerate([(first_in, first), (mid_in, mid), (twist_in, twist), (last_in, last)])
    ]

    def push(src, dst, phase, where):
        pltpu.make_async_remote_copy(
            src_ref=src,
            dst_ref=dst,
            send_sem=send_sems.at[phase],
            recv_sem=recv_sems.at[phase],
            device_id=where,
            device_id_type=MESH,
        ).start()

    def tell(semaphore, where):
        pl.semaphore_signal(semaphore, inc=1, device_id=where, device_id_type=MESH)

    def loop(low, high, step):
        def body(k, carry):
            step(k)
            return carry

        lax.fori_loop(low, high, body, 0)

    def others(low, high, step):
        def guarded(r):
            @pl.when(r != rank)
            def _():
                step(ranked(r))

        loop(low, high, guarded)

    def arrived(ref, count, phase):
        part = ref.at[pl.ds(0, count)]
        pltpu.make_async_copy(part, part, recv_sems.at[phase]).wait()

    def sent(ref, count, phase):
        part = ref.at[pl.ds(0, count)]
        pltpu.make_async_copy(part, part, send_sems.at[phase]).wait()

    for copy in inputs:
        copy.start()

    barrier = pltpu.get_barrier_semaphore()
    neighbour = {"ctx": me ^ 1, "ch": group}
    even_feats, odd_feats = feats.at[group], feats.at[groups + group]
    own_feats = pltpu.make_async_copy(feats_in, odd_feats, own_sem)

    def push_feats(src, which, other):
        pltpu.make_async_remote_copy(
            src_ref=src,
            dst_ref=feats.at[which * groups + group],
            send_sem=feat_sent.at[which, other],
            recv_sem=feat_sems.at[which, group],
            device_id={"ctx": 2 * chip + 1, "ch": other},
            device_id_type=MESH,
        ).start()

    def await_block(sems, which, other):
        part = feats.at[which * groups + other]
        pltpu.make_async_copy(part, part, sems.at[which, other]).wait()

    def await_feats(other):
        await_block(feat_sems, 0, other)
        await_block(feat_sems, 1, other)

    @pl.when(core == 1)
    def _():
        tell(barrier, neighbour)

        @pl.when(jnp.logical_not(at_hub))
        def _():
            tell(barrier, {"ctx": 2 * hub, "ch": group})

        def greet(other):
            tell(barrier, {"ctx": me, "ch": other})

            @pl.when(jnp.logical_not(at_hub))
            def _():
                tell(barrier, {"ctx": me - 1, "ch": other})

        others(jnp.where(kind < 2, wide * kind, groups), groups, greet)
        pl.semaphore_wait(barrier, greeters + jnp.where(at_hub, 1, 0))
        others(0, known, lambda other: push_feats(feats_in, 1, other))
        own_feats.start()
        for copy in tables:
            copy.start()

        @pl.when(at_hub)
        def _():
            tell(hello, neighbour)
            await_block(feat_sems, 0, group)
            others(0, known, lambda other: push_feats(even_feats, 0, other))

    @pl.when(jnp.logical_and(core == 0, at_hub))
    def _():
        tell(barrier, neighbour)
        pl.semaphore_wait(hello, 1)
        push_feats(feats_in, 0, group)

        pl.semaphore_wait(barrier, owners)
        loop(0, owners, lambda k: tell(ready, {"ctx": 2 * k + 1, "ch": group}))

    @pl.when(jnp.logical_and(core == 0, jnp.logical_not(at_hub)))
    def _():
        pl.semaphore_wait(barrier, greeters + 1)
        others(0, known, lambda other: push_feats(feats_in, 0, other))
        push_feats(feats_in, 0, group)

    for copy in inputs[:4]:
        copy.wait()
    key_vals, value_vals = key[...].astype(f32), value[...].astype(f32)
    gate_vals, up_vals = gate[...].astype(f32), upstream[...].astype(f32)
    mixed, inner = key_vals * value_vals, up_vals * gate_vals
    send_sig[:, 0, :] = mixed[:owners]
    send_sig[:, 1, :] = mixed[owners:]
    send_sig[:, 2, :] = inner[:owners]
    send_sig[:, 3, :] = inner[owners:]

    def push_sig(k):
        to = chip ^ k
        push(send_sig.at[to], recv_sig.at[me], 1, {"ctx": 2 * to + 1, "ch": group})

    @pl.when(core == 0)
    def _():
        @pl.when(jnp.logical_not(at_hub))
        def _():
            pl.semaphore_wait(ready, 1)

        loop(0, owners, push_sig)

    inputs[4].wait()

    @pl.when(core == 1)
    def _():
        recv_sig[pl.ds(me, 1)] = send_sig[pl.ds(chip, 1)]
        pl.semaphore_wait(ready, 1)
        loop(1, owners, push_sig)

        @pl.when(jnp.logical_not(at_hub))
        def _():
            await_block(feat_sems, 0, group)
            tell(ready, neighbour)

        eye = (
            lax.broadcasted_iota(jnp.int32, (2 * owners, 2 * owners), 0)
            == lax.broadcasted_iota(jnp.int32, (2 * owners, 2 * owners), 1)
        ).astype(f32)
        weight_t = dot_t(eye, weight[...])
        for copy in tables:
            copy.wait()
        cos, sin = twist[0], twist[1]
        rows = cos.shape[0]
        for n in range(2):
            high, low = halves(first[n])
            first_split[n] = jnp.concatenate([high, high, low], axis=1)
            last_split[2 * n], last_split[2 * n + 1] = halves(last[n])
            mid_split[2 * n], mid_split[2 * n + 1] = halves(mid[n])
        forward, backward = (mid_split[0], mid_split[1]), (mid_split[2], mid_split[3])
        lasts = [(last_split[0], last_split[1]), (last_split[2], last_split[3])]

        own_feats.wait()

        def push_both(other):
            push_feats(even_feats, 0, other)
            push_feats(odd_feats, 1, other)

        @pl.when(kind == 2)
        def _():
            pl.semaphore_wait(all_in, 1)
            others(known, groups, push_both)

        arrived(recv_sig, shards - 1, 1)
        specs = spectra([recv_sig[:, n, :] for n in range(4)], first_split[0], forward, cos, sin)
        mixed_specs = [specs[:rows], specs[rows : 2 * rows]]
        inner_specs = [specs[2 * rows : 3 * rows], specs[3 * rows :]]
        taps = signals_of(
            [times_conj(inner_specs[n], mixed_specs[n]) for n in range(2)], lasts[1], backward, cos, sin
        )
        send_taps[:, 0, :] = taps[:owners, :LANES]
        send_taps[:, 1, :] = taps[owners:, :LANES]
        send_taps[:, 2, :] = taps[:owners, LANES:]
        send_taps[:, 3, :] = taps[owners:, LANES:]

        def push_taps(k):
            to = chip ^ k
            push(send_taps.at[to], recv_taps.at[chip], 3, {"ctx": 2 * to + 1, "ch": group})

        loop(1, owners, push_taps)
        recv_taps[pl.ds(chip, 1)] = send_taps[pl.ds(chip, 1)]

        def trade(other):
            await_feats(other)
            push_both(other)

        @pl.when(kind < 2)
        def _():
            others(0, settled, await_feats)
            others(settled, groups, trade)

        @pl.when(jnp.logical_and(kind == 0, 2 * wide < groups))
        def _():
            for step in range(2, deep):
                tell(all_in, {"ctx": me, "ch": group + step})

        @pl.when(kind == 2)
        def _():
            others(0, known, await_feats)
            others(known, groups, await_feats)

        per = feats.shape[1]
        feats_all = jnp.concatenate(
            [
                feats[:groups].reshape(groups * per, LANES),
                feats[groups:].reshape(groups * per, LANES),
            ],
            axis=1,
        )
        filt = jnp.dot(weight_t, feats_all, precision=HIGHEST, preferred_element_type=f32) * scaling
        send_filt[:, 0, :] = filt[:owners, :LANES]
        send_filt[:, 1, :] = filt[:owners, LANES:]
        send_filt[:, 2, :] = filt[owners:, :LANES]
        send_filt[:, 3, :] = filt[owners:, LANES:]

        def push_filt(k):
            to = chip ^ k
            push(send_filt.at[to], recv_filt.at[chip], 2, {"ctx": 2 * to + 1, "ch": group})

        loop(1, owners, push_filt)
        recv_filt[pl.ds(chip, 1)] = send_filt[pl.ds(chip, 1)]

        def sent_odd(other):
            await_block(feat_sent, 1, other)

        others(0, groups, sent_odd)
        others(jnp.where(at_hub, 0, known), groups, lambda other: await_block(feat_sent, 0, other))

        arrived(recv_taps, owners - 1, 3)
        taps_here = jnp.concatenate(
            [
                jnp.concatenate([recv_taps[:, 0, :], recv_taps[:, 1, :]], axis=1),
                jnp.concatenate([recv_taps[:, 2, :], recv_taps[:, 3, :]], axis=1),
            ],
            axis=0,
        )
        part = dot_t(taps_here, feats_all)
        send_part[:, 0, :] = jnp.concatenate([part[:owners], part[owners:]], axis=1)

        def push_part(k):
            to = chip ^ k
            push(send_part.at[to], recv_part.at[chip], 5, {"ctx": 2 * to + 1, "ch": group})

        loop(1, owners, push_part)
        recv_part[pl.ds(chip, 1)] = send_part[pl.ds(chip, 1)]

        arrived(recv_filt, owners - 1, 2)
        filt_specs = spectra(
            [
                jnp.concatenate([recv_filt[:, 2 * n, :], recv_filt[:, 2 * n + 1, :]], axis=0)
                for n in range(2)
            ],
            first_split[1],
            forward,
            cos,
            sin,
        )
        filt_specs = [filt_specs[:rows], filt_specs[rows:]]
        results = signals_of(
            [times(mixed_specs[n], filt_specs[n]) for n in range(2)]
            + [times_conj(inner_specs[n], filt_specs[n]) for n in range(2)],
            lasts[0],
            backward,
            cos,
            sin,
        )
        for n in range(4):
            send_out[:, n, :] = results[:, n * LANES : (n + 1) * LANES]

        def push_out(k):
            to = me ^ k
            push(send_out.at[to], recv_out.at[chip], 4, {"ctx": to, "ch": group})

        loop(1, shards, push_out)
        recv_out[pl.ds(chip, 1)] = send_out[pl.ds(me, 1)]

        arrived(recv_part, owners - 1, 5)
        send_sum[pl.ds(0, 1)] = jnp.sum(recv_part[...], axis=0, keepdims=True) * (scaling * scaling)

        def push_sum(k):
            push(send_sum.at[0], recv_sum.at[chip], 6, {"ctx": me ^ k, "ch": group})

        loop(1, shards, push_sum)
        recv_sum[pl.ds(chip, 1)] = send_sum[pl.ds(0, 1)]
        arrived(recv_out, owners - 1, 4)
        sent(send_filt, owners - 1, 2)
        sent(send_taps, owners - 1, 3)
        sent(send_out, shards - 1, 4)
        sent(send_part, owners - 1, 5)
        sent(send_sig, owners - 1, 1)

    @pl.when(core == 0)
    def _():
        arrived(recv_out, owners, 4)
        await_block(feat_sent, 0, group)

        @pl.when(jnp.logical_not(at_hub))
        def _():
            others(0, known, lambda other: await_block(feat_sent, 0, other))

        sent(send_sig, owners, 1)

    @pl.when(core == 1)
    def _():
        arrived(recv_sum, owners - 1, 6)
        sent(send_sum, shards - 1, 6)

    @pl.when(core == 0)
    def _():
        arrived(recv_sum, owners, 6)


def finish(gate, key, value, upstream, out, total, output, gate_grad, key_grad, value_grad, weight_grad):
    conv = jnp.concatenate([out[:, 0, :], out[:, 1, :]], axis=0)
    mixed_grad = jnp.concatenate([out[:, 2, :], out[:, 3, :]], axis=0)
    output[...] = (gate[...].astype(f32) * conv).astype(bf16)
    gate_grad[...] = (upstream[...].astype(f32) * conv).astype(bf16)
    key_grad[...] = (mixed_grad * value[...].astype(f32)).astype(bf16)
    value_grad[...] = (mixed_grad * key[...].astype(f32)).astype(bf16)
    sums = total[:, 0, :]
    half = sums.shape[1] // 2
    grad_rows = jnp.concatenate([sums[:, :half], sums[:, half:]], axis=0)
    eye = (
        lax.broadcasted_iota(jnp.int32, (half, half), 0) == lax.broadcasted_iota(jnp.int32, (half, half), 1)
    ).astype(f32)
    weight_grad[...] = dot_t(eye, grad_rows)


def on_device(gate_input, key_input, value_input, features, filter_weight, out_grad):
    shards, groups = lax.axis_size("ctx"), lax.axis_size("ch")
    channels, length = gate_input.shape
    feat = filter_weight.shape[0]
    owners = shards // 2
    assert channels == 2 * owners and length == LANES and feat == LANES // 2
    tables = make_tables(shards)
    hbm = pl.BlockSpec(memory_space=pl.ANY)
    vmem = pl.BlockSpec(memory_space=pltpu.VMEM)
    rows = lambda count, width: pltpu.VMEM((count, width, LANES), f32)
    block = jax.ShapeDtypeStruct((channels, length), bf16)
    per = features.shape[0]
    out, total = pl.pallas_call(
        functools.partial(kernel, shards, groups),
        out_shape=(
            jax.ShapeDtypeStruct((owners, 4, LANES), f32),
            jax.ShapeDtypeStruct((owners, 1, LANES), f32),
        ),
        in_specs=[hbm] * 10,
        out_specs=(vmem,) * 2,
        scratch_shapes=[
            *[pltpu.VMEM((channels, length), bf16)] * 4,
            pltpu.VMEM(filter_weight.shape, f32),
            *[pltpu.VMEM(table.shape, f32) for table in tables],
            pltpu.VMEM((2, tables[0].shape[1], 3 * tables[0].shape[2]), bf16),
            pltpu.VMEM((4, *tables[1].shape[1:]), bf16),
            pltpu.VMEM((4, *tables[2].shape[1:]), bf16),
            rows(2 * groups, per),
            rows(owners, 4),
            rows(shards, 4),
            rows(owners, 4),
            rows(owners, 4),
            rows(owners, 4),
            rows(owners, 4),
            rows(owners, 1),
            rows(owners, 1),
            rows(shards, 1),
            rows(shards, 4),
            pltpu.SemaphoreType.DMA((5,)),
            pltpu.SemaphoreType.DMA((4,)),
            pltpu.SemaphoreType.DMA,
            pltpu.SemaphoreType.DMA((2, groups)),
            pltpu.SemaphoreType.DMA((2, groups)),
            pltpu.SemaphoreType.DMA((7,)),
            pltpu.SemaphoreType.DMA((7,)),
            pltpu.SemaphoreType.REGULAR,
            pltpu.SemaphoreType.REGULAR,
            pltpu.SemaphoreType.REGULAR,
        ],
        compiler_params=pltpu.CompilerParams(
            collective_id=0, has_side_effects=True, vmem_limit_bytes=56 * 1024 * 1024
        ),
    )(gate_input, key_input, value_input, features, filter_weight, out_grad, *tables)
    return pl.pallas_call(
        finish,
        out_shape=(block, block, block, block, jax.ShapeDtypeStruct((feat, channels), f32)),
        in_specs=[vmem] * 6,
        out_specs=(vmem,) * 5,
    )(gate_input, key_input, value_input, out_grad, out, total)


def solution(mesh):
    placed = (
        P("ch", "ctx"),
        P("ch", "ctx"),
        P("ch", "ctx"),
        P("ch", "ctx"),
        P(None, "ch"),
        P("ch", "ctx"),
    )
    return jax.shard_map(
        on_device,
        mesh=mesh,
        in_specs=placed,
        out_specs=(P("ch", "ctx"), P("ch", "ctx"), P("ch", "ctx"), P("ch", "ctx"), P(None, "ch")),
        check_vma=False,
    )
```

```python
import functools
import math

import jax
import jax.numpy as jnp
import numpy as np
from jax import lax
from jax.experimental import pallas as pl
from jax.experimental.pallas import tpu as pltpu
from jax.sharding import PartitionSpec as P

MESH = pl.DeviceIdType.MESH
HIGHEST = lax.Precision.HIGHEST
f32 = jnp.float32
bf16 = jnp.bfloat16
LANES = 128


def make_tables(shards):
    outer = 2 * shards
    padded = outer * LANES
    rows = -(-(shards + 1) // 8) * 8
    r = np.arange(rows)
    live = (r <= shards).astype(np.float64)
    natural = np.arange(shards)
    by_parity = np.concatenate([natural[0::2], natural[1::2]])

    def angles(left, right, period):
        return 2.0 * np.pi * ((left[:, None] * right[None, :]) % period) / period

    first, last = [], []
    weight = np.where((r == 0) | (r == shards), 1.0, 2.0) * live / padded
    for order in (natural, by_parity):
        turn = angles(r, order, outer)
        table = np.concatenate([np.cos(turn), np.sin(turn)], axis=0) * np.tile(live, 2)[:, None]
        first.append(table)
        turn = angles(order, r, outer)
        table = np.concatenate([np.cos(turn) * weight, -np.sin(turn) * weight], axis=1)
        last.append(table)
    q = np.arange(LANES)
    turn = angles(q, q, LANES)
    cos, sin = np.cos(turn), np.sin(turn)
    forward = np.block([[cos, -sin], [sin, cos]])
    backward = np.block([[cos, sin], [-sin, cos]])
    turn = angles(r, q, padded)
    twist = [np.cos(turn), np.sin(turn)]
    return tuple(np.stack(table).astype(np.float32) for table in (first, last, [forward, backward], twist))


def halves(x):
    high = x.astype(bf16)
    return high, (x - high.astype(f32)).astype(bf16)


def dot(a, b):
    return jnp.dot(a, b, preferred_element_type=f32)


def dot_t(a, b):
    return lax.dot_general(a, b, (((1,), (1,)), ((), ())), precision=HIGHEST, preferred_element_type=f32)


def spectra(signals, first, mid, cos, sin):
    rows = cos.shape[0]
    high, low = halves(jnp.concatenate(signals, axis=1))
    outer = dot(first, jnp.concatenate([high, low, high], axis=0))
    turned = []
    for index in range(len(signals)):
        part = outer[:, index * LANES : (index + 1) * LANES]
        along, across = part[:rows], part[rows:]
        turned.append(
            jnp.concatenate([along * cos - across * sin, -(across * cos + along * sin)], axis=1)
        )
    high, low = halves(jnp.concatenate(turned, axis=0))
    return dot(high, mid[0]) + dot(low, mid[0]) + dot(high, mid[1])


def signals_of(products, last, mid, cos, sin):
    rows = cos.shape[0]
    high, low = halves(jnp.concatenate(products, axis=0))
    inner = dot(high, mid[0]) + dot(low, mid[0]) + dot(high, mid[1])
    turned = []
    for index in range(len(products)):
        part = inner[index * rows : (index + 1) * rows]
        real, imag = part[:, :LANES], part[:, LANES:]
        turned.append(jnp.concatenate([real * cos - imag * sin, imag * cos + real * sin], axis=0))
    high, low = halves(jnp.concatenate(turned, axis=1))
    return dot(last[0], high) + dot(last[0], low) + dot(last[1], high)


def times(a, b):
    ar, ai, br, bi = a[:, :LANES], a[:, LANES:], b[:, :LANES], b[:, LANES:]
    return jnp.concatenate([ar * br - ai * bi, ar * bi + ai * br], axis=1)


def times_conj(a, b):
    ar, ai, br, bi = a[:, :LANES], a[:, LANES:], b[:, :LANES], b[:, LANES:]
    return jnp.concatenate([ar * br + ai * bi, ai * br - ar * bi], axis=1)


def kernel(
    shards,
    groups,
    gate_in,
    key_in,
    value_in,
    feats_in,
    weight_in,
    upstream_in,
    first_in,
    last_in,
    mid_in,
    twist_in,
    recv_out,
    recv_sum,
    gate,
    key,
    value,
    upstream,
    weight,
    first,
    last,
    mid,
    twist,
    first_split,
    last_split,
    mid_split,
    feats,
    feats_all,
    send_sig,
    recv_sig,
    send_filt,
    recv_filt,
    send_taps,
    recv_taps,
    send_part,
    recv_part,
    send_sum,
    send_out,
    in_sems,
    table_sems,
    own_sem,
    feat_sems,
    feat_sent,
    send_sems,
    recv_sems,
    hello,
    ready,
    all_in,
):
    me = lax.axis_index("ctx")
    group = lax.axis_index("ch")
    owners = shards // 2
    chip = me // 2
    core = me % 2
    scaling = 1.0 / math.sqrt(shards * LANES)
    deep = 4 if groups % 4 == 0 else 1
    wide = groups // deep
    rank = (group % deep) * wide + group // deep
    kind = jnp.minimum(group % deep, 2)
    known = wide * jnp.minimum(kind + 1, 2)
    settled = min(2 * wide, groups)
    greeters = known - jnp.where(kind < 2, 1, 0)
    hub = 1
    at_hub = chip == hub
    reducers = owners // 2
    reducer = jnp.logical_and(core == 1, jnp.logical_or(chip % 4 == 1, chip % 4 == 2))
    my_reducer = chip // 4 * 2 + chip % 4 - 1

    def ranked(r):
        return (r % wide) * deep + r // wide

    inputs = [
        pltpu.make_async_copy(src, dst, in_sems.at[n])
        for n, (src, dst) in enumerate(
            [(key_in, key), (value_in, value), (upstream_in, upstream), (gate_in, gate), (weight_in, weight)]
        )
    ]
    tables = [
        pltpu.make_async_copy(src, dst, table_sems.at[n])
        for n, (src, dst) in enumerate([(first_in, first), (mid_in, mid), (twist_in, twist), (last_in, last)])
    ]

    def push(src, dst, phase, where):
        pltpu.make_async_remote_copy(
            src_ref=src,
            dst_ref=dst,
            send_sem=send_sems.at[phase],
            recv_sem=recv_sems.at[phase],
            device_id=where,
            device_id_type=MESH,
        ).start()

    def tell(semaphore, where):
        pl.semaphore_signal(semaphore, inc=1, device_id=where, device_id_type=MESH)

    def loop(low, high, step):
        def body(k, carry):
            step(k)
            return carry

        lax.fori_loop(low, high, body, 0)

    def far_first(low, count, step):
        loop(count // 2, count, step)
        loop(low, count // 2, step)

    def others(low, high, step):
        def guarded(r):
            @pl.when(r != rank)
            def _():
                step(ranked(r))

        loop(low, high, guarded)

    def arrived(ref, count, phase):
        part = ref.at[pl.ds(0, count)]
        pltpu.make_async_copy(part, part, recv_sems.at[phase]).wait()

    def sent(ref, count, phase):
        part = ref.at[pl.ds(0, count)]
        pltpu.make_async_copy(part, part, send_sems.at[phase]).wait()

    for copy in inputs:
        copy.start()

    barrier = pltpu.get_barrier_semaphore()
    neighbour = {"ctx": me ^ 1, "ch": group}
    even_feats, odd_feats = feats.at[group], feats.at[groups + group]
    own_feats = pltpu.make_async_copy(feats_in, odd_feats, own_sem)

    def push_feats(src, which, other):
        pltpu.make_async_remote_copy(
            src_ref=src,
            dst_ref=feats.at[which * groups + group],
            send_sem=feat_sent.at[which, other],
            recv_sem=feat_sems.at[which, group],
            device_id={"ctx": 2 * chip + 1, "ch": other},
            device_id_type=MESH,
        ).start()

    def await_block(sems, which, other):
        part = feats.at[which * groups + other]
        pltpu.make_async_copy(part, part, sems.at[which, other]).wait()

    def await_feats(other):
        await_block(feat_sems, 0, other)
        await_block(feat_sems, 1, other)

    @pl.when(core == 1)
    def _():
        tell(barrier, neighbour)

        @pl.when(jnp.logical_not(at_hub))
        def _():
            tell(barrier, {"ctx": 2 * hub, "ch": group})

        def greet(other):
            tell(barrier, {"ctx": me, "ch": other})

            @pl.when(jnp.logical_not(at_hub))
            def _():
                tell(barrier, {"ctx": me - 1, "ch": other})

        others(jnp.where(kind < 2, wide * kind, groups), groups, greet)
        pl.semaphore_wait(barrier, greeters + jnp.where(at_hub, 1, 0))
        others(0, known, lambda other: push_feats(feats_in, 1, other))
        own_feats.start()
        for copy in tables:
            copy.start()

        @pl.when(at_hub)
        def _():
            tell(hello, neighbour)
            await_block(feat_sems, 0, group)
            others(0, known, lambda other: push_feats(even_feats, 0, other))

    @pl.when(jnp.logical_and(core == 0, at_hub))
    def _():
        tell(barrier, neighbour)
        pl.semaphore_wait(hello, 1)
        push_feats(feats_in, 0, group)

        pl.semaphore_wait(barrier, owners)
        loop(0, owners, lambda k: tell(ready, {"ctx": 2 * k + 1, "ch": group}))

    @pl.when(jnp.logical_and(core == 0, jnp.logical_not(at_hub)))
    def _():
        pl.semaphore_wait(barrier, greeters + 1)

        @pl.when(jnp.logical_not(at_hub))
        def _():
            tell(hello, neighbour)

        others(0, known, lambda other: push_feats(feats_in, 0, other))
        push_feats(feats_in, 0, group)

    for copy in inputs[:4]:
        copy.wait()
    key_vals, value_vals = key[...].astype(f32), value[...].astype(f32)
    gate_vals, up_vals = gate[...].astype(f32), upstream[...].astype(f32)
    mixed, inner = key_vals * value_vals, up_vals * gate_vals
    send_sig[:, 0, :] = mixed[:owners]
    send_sig[:, 1, :] = mixed[owners:]
    send_sig[:, 2, :] = inner[:owners]
    send_sig[:, 3, :] = inner[owners:]

    def push_sig(k):
        to = chip ^ k
        push(send_sig.at[to], recv_sig.at[me], 1, {"ctx": 2 * to + 1, "ch": group})

    @pl.when(core == 0)
    def _():
        @pl.when(jnp.logical_not(at_hub))
        def _():
            pl.semaphore_wait(ready, 1)

        far_first(0, owners, push_sig)

    inputs[4].wait()

    @pl.when(core == 1)
    def _():
        recv_sig[pl.ds(me, 1)] = send_sig[pl.ds(chip, 1)]
        pl.semaphore_wait(ready, 1)

        far_first(1, owners, push_sig)

        @pl.when(jnp.logical_not(at_hub))
        def _():
            pl.semaphore_wait(hello, 1)
            tell(ready, neighbour)

        eye = (
            lax.broadcasted_iota(jnp.int32, (2 * owners, 2 * owners), 0)
            == lax.broadcasted_iota(jnp.int32, (2 * owners, 2 * owners), 1)
        ).astype(f32)
        weight_t = dot_t(eye, weight[...])
        for copy in tables:
            copy.wait()
        cos, sin = twist[0], twist[1]
        rows = cos.shape[0]
        for n in range(2):
            high, low = halves(first[n])
            first_split[n] = jnp.concatenate([high, high, low], axis=1)
            last_split[2 * n], last_split[2 * n + 1] = halves(last[n])
            mid_split[2 * n], mid_split[2 * n + 1] = halves(mid[n])
        forward, backward = (mid_split[0], mid_split[1]), (mid_split[2], mid_split[3])
        lasts = [(last_split[0], last_split[1]), (last_split[2], last_split[3])]

        own_feats.wait()

        @pl.when(jnp.logical_not(at_hub))
        def _():
            await_block(feat_sems, 0, group)

        def push_both(other):
            push_feats(even_feats, 0, other)
            push_feats(odd_feats, 1, other)

        @pl.when(kind == 2)
        def _():
            pl.semaphore_wait(all_in, 1)
            others(known, groups, push_both)

        def trade(other):
            await_feats(other)
            push_both(other)

        def push_filt(k):
            to = chip ^ k
            push(send_filt.at[to], recv_filt.at[chip], 2, {"ctx": 2 * to + 1, "ch": group})

        def filter_phase():
            @pl.when(kind == 0)
            def _():
                others(2 * wide, groups, trade)

                @pl.when(2 * wide < groups)
                def _():
                    for step in range(2, deep):
                        tell(all_in, {"ctx": me, "ch": group + step})

            @pl.when(kind == 1)
            def _():
                others(0, settled, await_feats)
                others(settled, groups, trade)

            @pl.when(kind == 2)
            def _():
                others(0, groups, await_feats)

            per = feats.shape[1]
            feats_all[...] = jnp.concatenate(
                [
                    feats[:groups].reshape(groups * per, LANES),
                    feats[groups:].reshape(groups * per, LANES),
                ],
                axis=1,
            )
            filt = jnp.dot(weight_t, feats_all[...], precision=HIGHEST, preferred_element_type=f32) * scaling
            send_filt[:, 0, :] = filt[:owners, :LANES]
            send_filt[:, 1, :] = filt[:owners, LANES:]
            send_filt[:, 2, :] = filt[owners:, :LANES]
            send_filt[:, 3, :] = filt[owners:, LANES:]
            far_first(1, owners, push_filt)
            recv_filt[pl.ds(chip, 1)] = send_filt[pl.ds(chip, 1)]

        @pl.when(kind == 0)
        def _():
            others(0, wide, await_feats)
            others(wide, jnp.minimum(2 * wide, groups), trade)

        arrived(recv_sig, shards - 1, 1)
        specs = spectra([recv_sig[:, n, :] for n in range(4)], first_split[0], forward, cos, sin)
        mixed_specs = [specs[:rows], specs[rows : 2 * rows]]
        inner_specs = [specs[2 * rows : 3 * rows], specs[3 * rows :]]
        taps = signals_of(
            [times_conj(inner_specs[n], mixed_specs[n]) for n in range(2)], lasts[1], backward, cos, sin
        )
        send_taps[:, 0, :] = taps[:owners, :LANES]
        send_taps[:, 1, :] = taps[owners:, :LANES]
        send_taps[:, 2, :] = taps[:owners, LANES:]
        send_taps[:, 3, :] = taps[owners:, LANES:]

        def push_taps(k):
            to = chip ^ k
            push(send_taps.at[to], recv_taps.at[chip], 3, {"ctx": 2 * to + 1, "ch": group})

        far_first(1, owners, push_taps)
        recv_taps[pl.ds(chip, 1)] = send_taps[pl.ds(chip, 1)]

        filter_phase()

        arrived(recv_taps, owners - 1, 3)
        taps_here = jnp.concatenate(
            [
                jnp.concatenate([recv_taps[:, 0, :], recv_taps[:, 1, :]], axis=1),
                jnp.concatenate([recv_taps[:, 2, :], recv_taps[:, 3, :]], axis=1),
            ],
            axis=0,
        )
        part = dot_t(taps_here, feats_all[...])
        pairs = jnp.concatenate([part[:owners], part[owners:]], axis=1)
        send_part[:, 0, :] = pairs[:reducers]
        send_part[:, 1, :] = pairs[reducers:]

        def push_part(k):
            @pl.when(jnp.logical_not(jnp.logical_and(reducer, k == my_reducer)))
            def _():
                to = k // 2 * 4 + 1 + k % 2
                push(send_part.at[k], recv_part.at[chip], 5, {"ctx": 2 * to + 1, "ch": group})

        loop(0, reducers, push_part)

        @pl.when(reducer)
        def _():
            recv_part[pl.ds(chip, 1)] = send_part[pl.ds(my_reducer, 1)]

        arrived(recv_filt, owners - 1, 2)
        filt_specs = spectra(
            [
                jnp.concatenate([recv_filt[:, 2 * n, :], recv_filt[:, 2 * n + 1, :]], axis=0)
                for n in range(2)
            ],
            first_split[1],
            forward,
            cos,
            sin,
        )
        filt_specs = [filt_specs[:rows], filt_specs[rows:]]
        results = signals_of(
            [times(mixed_specs[n], filt_specs[n]) for n in range(2)]
            + [times_conj(inner_specs[n], filt_specs[n]) for n in range(2)],
            lasts[0],
            backward,
            cos,
            sin,
        )
        for n in range(4):
            send_out[:, n, :] = results[:, n * LANES : (n + 1) * LANES]

        def push_out(k):
            to = me ^ k
            push(send_out.at[to], recv_out.at[chip], 4, {"ctx": to, "ch": group})

        far_first(1, shards, push_out)
        recv_out[pl.ds(chip, 1)] = send_out[pl.ds(me, 1)]

        def sent_odd(other):
            await_block(feat_sent, 1, other)

        others(0, groups, sent_odd)
        others(jnp.where(at_hub, 0, known), groups, lambda other: await_block(feat_sent, 0, other))
        sent(send_filt, owners - 1, 2)
        sent(send_taps, owners - 1, 3)
        sent(send_sig, owners - 1, 1)

        @pl.when(reducer)
        def _():
            arrived(recv_part, owners - 1, 5)
            send_sum[pl.ds(0, 1)] = jnp.sum(recv_part[...], axis=0, keepdims=True) * (scaling * scaling)

            def push_sum(k):
                push(send_sum.at[0], recv_sum.at[my_reducer], 6, {"ctx": me ^ k, "ch": group})

            far_first(1, shards, push_sum)
            recv_sum[pl.ds(my_reducer, 1)] = send_sum[pl.ds(0, 1)]
            sent(send_part, reducers - 1, 5)

        @pl.when(jnp.logical_not(reducer))
        def _():
            sent(send_part, reducers, 5)

        arrived(recv_out, owners - 1, 4)
        sent(send_out, shards - 1, 4)

    @pl.when(core == 0)
    def _():
        arrived(recv_out, owners, 4)
        await_block(feat_sent, 0, group)

        @pl.when(jnp.logical_not(at_hub))
        def _():
            others(0, known, lambda other: await_block(feat_sent, 0, other))

        sent(send_sig, owners, 1)

    @pl.when(core == 1)
    def _():
        @pl.when(reducer)
        def _():
            arrived(recv_sum, reducers - 1, 6)
            sent(send_sum, shards - 1, 6)

        @pl.when(jnp.logical_not(reducer))
        def _():
            arrived(recv_sum, reducers, 6)

    @pl.when(core == 0)
    def _():
        arrived(recv_sum, reducers, 6)


def finish(*refs):
    sources, targets = refs[:6], refs[6:11]
    gate, key, value, upstream, out, total = refs[11:17]
    results = refs[17:22]
    in_sems, out_sems = refs[22:]
    loads = [
        pltpu.make_async_copy(source, ref, in_sems.at[n])
        for n, (source, ref) in enumerate(zip(sources, (gate, key, value, upstream, out, total)))
    ]
    stores = [
        pltpu.make_async_copy(ref, target, out_sems.at[n]) for n, (ref, target) in enumerate(zip(results, targets))
    ]
    for n in (4, 0, 3, 1, 2, 5):
        loads[n].start()
    loads[4].wait()
    conv = jnp.concatenate([out[:, 0, :], out[:, 1, :]], axis=0)
    mixed_grad = jnp.concatenate([out[:, 2, :], out[:, 3, :]], axis=0)
    for n, (load, ref, factor) in enumerate(
        [(0, gate, conv), (3, upstream, conv), (2, value, mixed_grad), (1, key, mixed_grad)]
    ):
        loads[load].wait()
        results[n][...] = (ref[...].astype(f32) * factor).astype(bf16)
        stores[n].start()
    loads[5].wait()
    sums = jnp.concatenate([total[:, 0, :], total[:, 1, :]], axis=0)
    half = sums.shape[1] // 2
    grad_rows = jnp.concatenate([sums[:, :half], sums[:, half:]], axis=0)
    eye = (
        lax.broadcasted_iota(jnp.int32, (half, half), 0) == lax.broadcasted_iota(jnp.int32, (half, half), 1)
    ).astype(f32)
    results[4][...] = dot_t(eye, grad_rows)
    stores[4].start()
    for store in stores:
        store.wait()


def on_device(gate_input, key_input, value_input, features, filter_weight, out_grad):
    shards, groups = lax.axis_size("ctx"), lax.axis_size("ch")
    channels, length = gate_input.shape
    feat = filter_weight.shape[0]
    owners = shards // 2
    reducers = owners // 2
    assert channels == 2 * owners and length == LANES and feat == LANES // 2
    tables = make_tables(shards)
    hbm = pl.BlockSpec(memory_space=pl.ANY)
    vmem = pl.BlockSpec(memory_space=pltpu.VMEM)
    rows = lambda count, width: pltpu.VMEM((count, width, LANES), f32)
    block = jax.ShapeDtypeStruct((channels, length), bf16)
    per = features.shape[0]
    out, total = pl.pallas_call(
        functools.partial(kernel, shards, groups),
        out_shape=(
            jax.ShapeDtypeStruct((owners, 4, LANES), f32),
            jax.ShapeDtypeStruct((reducers, 2, LANES), f32),
        ),
        in_specs=[hbm] * 10,
        out_specs=(vmem,) * 2,
        scratch_shapes=[
            *[pltpu.VMEM((channels, length), bf16)] * 4,
            pltpu.VMEM(filter_weight.shape, f32),
            *[pltpu.VMEM(table.shape, f32) for table in tables],
            pltpu.VMEM((2, tables[0].shape[1], 3 * tables[0].shape[2]), bf16),
            pltpu.VMEM((4, *tables[1].shape[1:]), bf16),
            pltpu.VMEM((4, *tables[2].shape[1:]), bf16),
            rows(2 * groups, per),
            pltpu.VMEM((feat, 2 * LANES), f32),
            rows(owners, 4),
            rows(shards, 4),
            rows(owners, 4),
            rows(owners, 4),
            rows(owners, 4),
            rows(owners, 4),
            rows(reducers, 2),
            rows(owners, 2),
            rows(shards, 2),
            rows(shards, 4),
            pltpu.SemaphoreType.DMA((5,)),
            pltpu.SemaphoreType.DMA((4,)),
            pltpu.SemaphoreType.DMA,
            pltpu.SemaphoreType.DMA((2, groups)),
            pltpu.SemaphoreType.DMA((2, groups)),
            pltpu.SemaphoreType.DMA((7,)),
            pltpu.SemaphoreType.DMA((7,)),
            pltpu.SemaphoreType.REGULAR,
            pltpu.SemaphoreType.REGULAR,
            pltpu.SemaphoreType.REGULAR,
        ],
        compiler_params=pltpu.CompilerParams(
            collective_id=0, has_side_effects=True, vmem_limit_bytes=56 * 1024 * 1024
        ),
    )(gate_input, key_input, value_input, features, filter_weight, out_grad, *tables)
    return pl.pallas_call(
        finish,
        out_shape=(block, block, block, block, jax.ShapeDtypeStruct((feat, channels), f32)),
        in_specs=[hbm] * 6,
        out_specs=(hbm,) * 5,
        scratch_shapes=[
            *[pltpu.VMEM((channels, length), bf16)] * 4,
            rows(owners, 4),
            rows(reducers, 2),
            *[pltpu.VMEM((channels, length), bf16)] * 4,
            pltpu.VMEM((feat, channels), f32),
            pltpu.SemaphoreType.DMA((6,)),
            pltpu.SemaphoreType.DMA((5,)),
        ],
        compiler_params=pltpu.CompilerParams(vmem_limit_bytes=56 * 1024 * 1024),
    )(gate_input, key_input, value_input, out_grad, out, total)


def solution(mesh):
    placed = (
        P("ch", "ctx"),
        P("ch", "ctx"),
        P("ch", "ctx"),
        P("ch", "ctx"),
        P(None, "ch"),
        P("ch", "ctx"),
    )
    return jax.shard_map(
        on_device,
        mesh=mesh,
        in_specs=placed,
        out_specs=(P("ch", "ctx"), P("ch", "ctx"), P("ch", "ctx"), P("ch", "ctx"), P(None, "ch")),
        check_vma=False,
    )
```

```python
import functools
import math

import jax
import jax.numpy as jnp
import numpy as np
from jax import lax
from jax.experimental import pallas as pl
from jax.experimental.pallas import tpu as pltpu
from jax.sharding import PartitionSpec as P

MESH = pl.DeviceIdType.MESH
HIGHEST = lax.Precision.HIGHEST
f32 = jnp.float32
bf16 = jnp.bfloat16
LANES = 128


def make_tables(shards):
    outer = 2 * shards
    padded = outer * LANES
    rows = -(-(shards + 1) // 8) * 8
    r = np.arange(rows)
    live = (r <= shards).astype(np.float64)
    natural = np.arange(shards)
    by_parity = np.concatenate([natural[0::2], natural[1::2]])

    def angles(left, right, period):
        return 2.0 * np.pi * ((left[:, None] * right[None, :]) % period) / period

    first, last = [], []
    weight = np.where((r == 0) | (r == shards), 1.0, 2.0) * live / padded
    for order in (natural, by_parity):
        turn = angles(r, order, outer)
        table = np.concatenate([np.cos(turn), np.sin(turn)], axis=0) * np.tile(live, 2)[:, None]
        first.append(table)
        turn = angles(order, r, outer)
        table = np.concatenate([np.cos(turn) * weight, -np.sin(turn) * weight], axis=1)
        last.append(table)
    q = np.arange(LANES)
    turn = angles(q, q, LANES)
    cos, sin = np.cos(turn), np.sin(turn)
    forward = np.block([[cos, -sin], [sin, cos]])
    backward = np.block([[cos, sin], [-sin, cos]])
    turn = angles(r, q, padded)
    twist = [np.cos(turn), np.sin(turn)]
    return tuple(np.stack(table).astype(np.float32) for table in (first, last, [forward, backward], twist))


def halves(x):
    high = x.astype(bf16)
    return high, (x - high.astype(f32)).astype(bf16)


def dot(a, b):
    return jnp.dot(a, b, preferred_element_type=f32)


def rows_by_rows(a, b):
    return lax.dot_general(a, b, (((1,), (1,)), ((), ())), preferred_element_type=f32)


def dot_t(a, b):
    return lax.dot_general(a, b, (((1,), (1,)), ((), ())), precision=HIGHEST, preferred_element_type=f32)


def spectra(signals, first, mid, cos, sin):
    rows = cos.shape[0]
    high, low = halves(jnp.concatenate(signals, axis=1))
    outer = dot(first, jnp.concatenate([high, low, high], axis=0))
    turned = []
    for index in range(len(signals)):
        part = outer[:, index * LANES : (index + 1) * LANES]
        along, across = part[:rows], part[rows:]
        turned.append(
            jnp.concatenate([along * cos - across * sin, -(across * cos + along * sin)], axis=1)
        )
    high, low = halves(jnp.concatenate(turned, axis=0))
    return dot(high, mid[0]) + dot(low, mid[0]) + dot(high, mid[1])


def signals_of(products, last, mid, cos, sin):
    rows = cos.shape[0]
    high, low = halves(jnp.concatenate(products, axis=0))
    inner = dot(high, mid[0]) + dot(low, mid[0]) + dot(high, mid[1])
    turned = []
    for index in range(len(products)):
        part = inner[index * rows : (index + 1) * rows]
        real, imag = part[:, :LANES], part[:, LANES:]
        turned.append(jnp.concatenate([real * cos - imag * sin, imag * cos + real * sin], axis=0))
    high, low = halves(jnp.concatenate(turned, axis=1))
    return dot(last[0], high) + dot(last[0], low) + dot(last[1], high)


def times(a, b):
    ar, ai, br, bi = a[:, :LANES], a[:, LANES:], b[:, :LANES], b[:, LANES:]
    return jnp.concatenate([ar * br - ai * bi, ar * bi + ai * br], axis=1)


def times_conj(a, b):
    ar, ai, br, bi = a[:, :LANES], a[:, LANES:], b[:, :LANES], b[:, LANES:]
    return jnp.concatenate([ar * br + ai * bi, ai * br - ar * bi], axis=1)


def kernel(
    shards,
    groups,
    gate_in,
    key_in,
    value_in,
    feats_in,
    weight_in,
    upstream_in,
    first_in,
    last_in,
    mid_in,
    twist_in,
    output_hbm,
    gate_grad_hbm,
    key_grad_hbm,
    value_grad_hbm,
    weight_grad_hbm,
    output,
    gate_grad,
    key_grad,
    value_grad,
    weight_grad,
    recv_out,
    recv_sum,
    gate,
    key,
    value,
    upstream,
    weight,
    first,
    last,
    mid,
    twist,
    first_split,
    last_split,
    mid_split,
    feats,
    feats_all,
    send_sig,
    recv_sig,
    send_filt,
    recv_filt,
    send_taps,
    recv_taps,
    send_part,
    recv_part,
    send_sum,
    send_out,
    in_sems,
    out_sems,
    table_sems,
    own_sem,
    feat_sems,
    feat_sent,
    send_sems,
    recv_sems,
    hello,
    ready,
    all_in,
):
    me = lax.axis_index("ctx")
    group = lax.axis_index("ch")
    owners = shards // 2
    chip = me // 2
    core = me % 2
    scaling = 1.0 / math.sqrt(shards * LANES)
    deep = 4 if groups % 4 == 0 else 1
    wide = groups // deep
    rank = (group % deep) * wide + group // deep
    kind = jnp.minimum(group % deep, 2)
    known = wide * jnp.minimum(kind + 1, 2)
    settled = min(2 * wide, groups)
    greeters = known - jnp.where(kind < 2, 1, 0)
    hub = 1
    at_hub = chip == hub
    reducers = owners // 4
    ring = owners // 4
    along = chip // 4
    nearness = jnp.where(
        along < 2, along, jnp.where(along == ring - 1, 2, jnp.where(along == 2, 3, reducers))
    )
    my_reducer = nearness * 2 + chip % 4
    reducer = jnp.logical_and(core == 1, jnp.logical_and(chip % 4 < 2, my_reducer < reducers))

    def reducer_chip(k):
        near = k // 2
        return jnp.where(near == 2, ring - 1, jnp.where(near == 3, 2, near)) * 4 + k % 2

    def ranked(r):
        return (r % wide) * deep + r // wide

    inputs = [
        pltpu.make_async_copy(src, dst, in_sems.at[n])
        for n, (src, dst) in enumerate(
            [(key_in, key), (value_in, value), (upstream_in, upstream), (gate_in, gate), (weight_in, weight)]
        )
    ]
    tables = [
        pltpu.make_async_copy(src, dst, table_sems.at[n])
        for n, (src, dst) in enumerate([(first_in, first), (mid_in, mid), (twist_in, twist), (last_in, last)])
    ]

    def push(src, dst, phase, where):
        pltpu.make_async_remote_copy(
            src_ref=src,
            dst_ref=dst,
            send_sem=send_sems.at[phase],
            recv_sem=recv_sems.at[phase],
            device_id=where,
            device_id_type=MESH,
        ).start()

    def tell(semaphore, where):
        pl.semaphore_signal(semaphore, inc=1, device_id=where, device_id_type=MESH)

    def loop(low, high, step):
        def body(k, carry):
            step(k)
            return carry

        lax.fori_loop(low, high, body, 0)

    def far_first(low, count, step):
        loop(count // 2, count, step)
        loop(low, count // 2, step)

    def others(low, high, step):
        def guarded(r):
            @pl.when(r != rank)
            def _():
                step(ranked(r))

        loop(low, high, guarded)

    def arrived(ref, count, phase):
        part = ref.at[pl.ds(0, count)]
        pltpu.make_async_copy(part, part, recv_sems.at[phase]).wait()

    def sent(ref, count, phase):
        part = ref.at[pl.ds(0, count)]
        pltpu.make_async_copy(part, part, send_sems.at[phase]).wait()

    for copy in inputs:
        copy.start()

    barrier = pltpu.get_barrier_semaphore()
    neighbour = {"ctx": me ^ 1, "ch": group}
    even_feats, odd_feats = feats.at[group], feats.at[groups + group]
    own_feats = pltpu.make_async_copy(feats_in, odd_feats, own_sem)

    def push_feats(src, which, other):
        pltpu.make_async_remote_copy(
            src_ref=src,
            dst_ref=feats.at[which * groups + group],
            send_sem=feat_sent.at[which, other],
            recv_sem=feat_sems.at[which, group],
            device_id={"ctx": 2 * chip + 1, "ch": other},
            device_id_type=MESH,
        ).start()

    def await_block(sems, which, other):
        part = feats.at[which * groups + other]
        pltpu.make_async_copy(part, part, sems.at[which, other]).wait()

    def await_feats(other):
        await_block(feat_sems, 0, other)
        await_block(feat_sems, 1, other)

    @pl.when(core == 1)
    def _():
        tell(barrier, neighbour)

        @pl.when(jnp.logical_not(at_hub))
        def _():
            tell(barrier, {"ctx": 2 * hub, "ch": group})

        def greet(other):
            tell(barrier, {"ctx": me, "ch": other})

            @pl.when(jnp.logical_not(at_hub))
            def _():
                tell(barrier, {"ctx": me - 1, "ch": other})

        others(jnp.where(kind < 2, wide * kind, groups), groups, greet)
        pl.semaphore_wait(barrier, greeters + jnp.where(at_hub, 1, 0))
        others(0, known, lambda other: push_feats(feats_in, 1, other))
        own_feats.start()
        for copy in tables:
            copy.start()

        @pl.when(at_hub)
        def _():
            tell(hello, neighbour)
            await_block(feat_sems, 0, group)
            others(0, known, lambda other: push_feats(even_feats, 0, other))

    @pl.when(jnp.logical_and(core == 0, at_hub))
    def _():
        tell(barrier, neighbour)
        pl.semaphore_wait(hello, 1)
        push_feats(feats_in, 0, group)

        pl.semaphore_wait(barrier, owners)
        loop(0, owners, lambda k: tell(ready, {"ctx": 2 * k + 1, "ch": group}))

    @pl.when(jnp.logical_and(core == 0, jnp.logical_not(at_hub)))
    def _():
        pl.semaphore_wait(barrier, greeters + 1)

        @pl.when(jnp.logical_not(at_hub))
        def _():
            tell(hello, neighbour)

        others(0, known, lambda other: push_feats(feats_in, 0, other))
        push_feats(feats_in, 0, group)

    for copy in inputs[:4]:
        copy.wait()
    key_vals, value_vals = key[...].astype(f32), value[...].astype(f32)
    gate_vals, up_vals = gate[...].astype(f32), upstream[...].astype(f32)
    mixed, inner = key_vals * value_vals, up_vals * gate_vals
    send_sig[:, 0, :] = mixed[:owners]
    send_sig[:, 1, :] = mixed[owners:]
    send_sig[:, 2, :] = inner[:owners]
    send_sig[:, 3, :] = inner[owners:]

    def push_sig(k):
        to = chip ^ k
        push(send_sig.at[to], recv_sig.at[me], 1, {"ctx": 2 * to + 1, "ch": group})

    @pl.when(core == 0)
    def _():
        @pl.when(jnp.logical_not(at_hub))
        def _():
            pl.semaphore_wait(ready, 1)

        far_first(0, owners, push_sig)

    inputs[4].wait()

    @pl.when(core == 1)
    def _():
        recv_sig[pl.ds(me, 1)] = send_sig[pl.ds(chip, 1)]
        pl.semaphore_wait(ready, 1)

        far_first(1, owners, push_sig)

        @pl.when(jnp.logical_not(at_hub))
        def _():
            pl.semaphore_wait(hello, 1)
            tell(ready, neighbour)

        eye = (
            lax.broadcasted_iota(jnp.int32, (2 * owners, 2 * owners), 0)
            == lax.broadcasted_iota(jnp.int32, (2 * owners, 2 * owners), 1)
        ).astype(f32)
        high, low = halves(dot_t(eye, weight[...]) * scaling)
        weight_t = jnp.concatenate([high, high, low], axis=1)
        for copy in tables:
            copy.wait()
        cos, sin = twist[0], twist[1]
        rows = cos.shape[0]
        for n in range(2):
            high, low = halves(first[n])
            first_split[n] = jnp.concatenate([high, high, low], axis=1)
            last_split[2 * n], last_split[2 * n + 1] = halves(last[n])
            mid_split[2 * n], mid_split[2 * n + 1] = halves(mid[n])
        forward, backward = (mid_split[0], mid_split[1]), (mid_split[2], mid_split[3])
        lasts = [(last_split[0], last_split[1]), (last_split[2], last_split[3])]

        own_feats.wait()

        @pl.when(jnp.logical_not(at_hub))
        def _():
            await_block(feat_sems, 0, group)

        def push_both(other):
            push_feats(even_feats, 0, other)
            push_feats(odd_feats, 1, other)

        @pl.when(kind == 2)
        def _():
            pl.semaphore_wait(all_in, 1)
            others(known, groups, push_both)

        def trade(other):
            await_feats(other)
            push_both(other)

        def push_filt(k):
            to = chip ^ k
            push(send_filt.at[to], recv_filt.at[chip], 2, {"ctx": 2 * to + 1, "ch": group})

        def filter_phase():
            @pl.when(kind == 0)
            def _():
                others(3 * wide, groups, trade)
                others(2 * wide, min(3 * wide, groups), trade)

                @pl.when(2 * wide < groups)
                def _():
                    for step in range(2, deep):
                        tell(all_in, {"ctx": me, "ch": group + step})

            @pl.when(kind == 1)
            def _():
                others(0, settled, await_feats)
                others(settled, groups, trade)

            @pl.when(kind == 2)
            def _():
                others(0, groups, await_feats)

            per = feats.shape[1]
            feats_all[...] = jnp.concatenate(
                [
                    feats[:groups].reshape(groups * per, LANES),
                    feats[groups:].reshape(groups * per, LANES),
                ],
                axis=1,
            )
            high, low = halves(feats_all[...])
            filt = dot(weight_t, jnp.concatenate([high, low, high], axis=0))
            send_filt[:, 0, :] = filt[:owners, :LANES]
            send_filt[:, 1, :] = filt[:owners, LANES:]
            send_filt[:, 2, :] = filt[owners:, :LANES]
            send_filt[:, 3, :] = filt[owners:, LANES:]
            far_first(1, owners, push_filt)
            recv_filt[pl.ds(chip, 1)] = send_filt[pl.ds(chip, 1)]

        @pl.when(kind == 0)
        def _():
            others(0, wide, await_feats)
            others(wide, jnp.minimum(2 * wide, groups), trade)

        arrived(recv_sig, shards - 1, 1)
        specs = spectra([recv_sig[:, n, :] for n in range(4)], first_split[0], forward, cos, sin)
        mixed_specs = [specs[:rows], specs[rows : 2 * rows]]
        inner_specs = [specs[2 * rows : 3 * rows], specs[3 * rows :]]
        taps = signals_of(
            [times_conj(inner_specs[n], mixed_specs[n]) for n in range(2)], lasts[1], backward, cos, sin
        )
        send_taps[:, 0, :] = taps[:owners, :LANES]
        send_taps[:, 1, :] = taps[owners:, :LANES]
        send_taps[:, 2, :] = taps[:owners, LANES:]
        send_taps[:, 3, :] = taps[owners:, LANES:]

        def push_taps(k):
            to = chip ^ k
            push(send_taps.at[to], recv_taps.at[chip], 3, {"ctx": 2 * to + 1, "ch": group})

        far_first(1, owners, push_taps)
        recv_taps[pl.ds(chip, 1)] = send_taps[pl.ds(chip, 1)]

        filter_phase()

        arrived(recv_taps, owners - 1, 3)
        taps_here = jnp.concatenate(
            [
                jnp.concatenate([recv_taps[:, 0, :], recv_taps[:, 1, :]], axis=1),
                jnp.concatenate([recv_taps[:, 2, :], recv_taps[:, 3, :]], axis=1),
            ],
            axis=0,
        )
        feats_high, feats_low = halves(feats_all[...])
        high, low = halves(taps_here)
        part = rows_by_rows(high, feats_high) + rows_by_rows(low, feats_high) + rows_by_rows(high, feats_low)
        pairs = jnp.concatenate([part[:owners], part[owners:]], axis=1)
        for n in range(4):
            send_part[:, n, :] = pairs[n * reducers : (n + 1) * reducers]

        def push_part(k):
            @pl.when(jnp.logical_not(jnp.logical_and(reducer, k == my_reducer)))
            def _():
                push(send_part.at[k], recv_part.at[chip], 5, {"ctx": 2 * reducer_chip(k) + 1, "ch": group})

        loop(0, reducers, push_part)

        @pl.when(reducer)
        def _():
            recv_part[pl.ds(chip, 1)] = send_part[pl.ds(my_reducer, 1)]

        arrived(recv_filt, owners - 1, 2)
        filt_specs = spectra(
            [
                jnp.concatenate([recv_filt[:, 2 * n, :], recv_filt[:, 2 * n + 1, :]], axis=0)
                for n in range(2)
            ],
            first_split[1],
            forward,
            cos,
            sin,
        )
        filt_specs = [filt_specs[:rows], filt_specs[rows:]]
        results = signals_of(
            [times(mixed_specs[n], filt_specs[n]) for n in range(2)]
            + [times_conj(inner_specs[n], filt_specs[n]) for n in range(2)],
            lasts[0],
            backward,
            cos,
            sin,
        )
        for n in range(4):
            send_out[:, n, :] = results[:, n * LANES : (n + 1) * LANES]

        def push_out(k):
            to = me ^ k
            push(send_out.at[to], recv_out.at[chip], 4, {"ctx": to, "ch": group})

        far_first(1, shards, push_out)
        recv_out[pl.ds(chip, 1)] = send_out[pl.ds(me, 1)]

        @pl.when(reducer)
        def _():
            arrived(recv_part, owners - 1, 5)
            send_sum[pl.ds(0, 1)] = jnp.sum(recv_part[...], axis=0, keepdims=True) * (scaling * scaling)

            def push_sum(k):
                push(send_sum.at[0], recv_sum.at[my_reducer], 6, {"ctx": me ^ k, "ch": group})

            far_first(1, shards, push_sum)
            recv_sum[pl.ds(my_reducer, 1)] = send_sum[pl.ds(0, 1)]
            sent(send_part, reducers - 1, 5)

        @pl.when(jnp.logical_not(reducer))
        def _():
            sent(send_part, reducers, 5)

        def sent_odd(other):
            await_block(feat_sent, 1, other)

        others(0, groups, sent_odd)
        others(jnp.where(at_hub, 0, known), groups, lambda other: await_block(feat_sent, 0, other))
        sent(send_filt, owners - 1, 2)
        sent(send_taps, owners - 1, 3)
        sent(send_sig, owners - 1, 1)
        arrived(recv_out, owners - 1, 4)
        sent(send_out, shards - 1, 4)

    @pl.when(core == 0)
    def _():
        await_block(feat_sent, 0, group)

        @pl.when(jnp.logical_not(at_hub))
        def _():
            others(0, known, lambda other: await_block(feat_sent, 0, other))

        sent(send_sig, owners, 1)
        arrived(recv_out, owners, 4)

    results = [
        pltpu.make_async_copy(ref, target, out_sems.at[n])
        for n, (ref, target) in enumerate(
            [
                (output, output_hbm),
                (gate_grad, gate_grad_hbm),
                (key_grad, key_grad_hbm),
                (value_grad, value_grad_hbm),
                (weight_grad, weight_grad_hbm),
            ]
        )
    ]
    conv = jnp.concatenate([recv_out[:, 0, :], recv_out[:, 1, :]], axis=0)
    output[...] = (gate[...].astype(f32) * conv).astype(bf16)
    results[0].start()
    gate_grad[...] = (upstream[...].astype(f32) * conv).astype(bf16)
    results[1].start()
    mixed_grad = jnp.concatenate([recv_out[:, 2, :], recv_out[:, 3, :]], axis=0)
    key_grad[...] = (mixed_grad * value[...].astype(f32)).astype(bf16)
    results[2].start()
    value_grad[...] = (mixed_grad * key[...].astype(f32)).astype(bf16)
    results[3].start()

    @pl.when(reducer)
    def _():
        arrived(recv_sum, reducers - 1, 6)

    @pl.when(jnp.logical_not(reducer))
    def _():
        arrived(recv_sum, reducers, 6)

    sums = jnp.concatenate([recv_sum[:, n, :] for n in range(4)], axis=0)
    half = sums.shape[1] // 2
    eye = (
        lax.broadcasted_iota(jnp.int32, (half, half), 0) == lax.broadcasted_iota(jnp.int32, (half, half), 1)
    ).astype(bf16)
    high, low = halves(jnp.concatenate([sums[:, :half], sums[:, half:]], axis=0))
    weight_grad[...] = rows_by_rows(eye, high) + rows_by_rows(eye, low)
    results[4].start()

    @pl.when(reducer)
    def _():
        sent(send_sum, shards - 1, 6)

    for copy in results:
        copy.wait()


def hand_over(*refs):
    sources, targets, held = refs[:5], refs[5:10], refs[10:15]
    in_sems, out_sems = refs[15:]
    loads = [pltpu.make_async_copy(source, ref, in_sems.at[n]) for n, (source, ref) in enumerate(zip(sources, held))]
    stores = [pltpu.make_async_copy(ref, target, out_sems.at[n]) for n, (ref, target) in enumerate(zip(held, targets))]
    for load in loads:
        load.start()
    for load, store in zip(loads, stores):
        load.wait()
        store.start()
    for store in stores:
        store.wait()


def on_device(gate_input, key_input, value_input, features, filter_weight, out_grad):
    shards, groups = lax.axis_size("ctx"), lax.axis_size("ch")
    channels, length = gate_input.shape
    feat = filter_weight.shape[0]
    owners = shards // 2
    reducers = owners // 4
    assert channels == 2 * owners and length == LANES and feat == LANES // 2
    tables = make_tables(shards)
    hbm = pl.BlockSpec(memory_space=pl.ANY)
    rows = lambda count, width: pltpu.VMEM((count, width, LANES), f32)
    block = jax.ShapeDtypeStruct((channels, length), bf16)
    per = features.shape[0]
    shapes = (block, block, block, block, jax.ShapeDtypeStruct((feat, channels), f32))
    results = pl.pallas_call(
        functools.partial(kernel, shards, groups),
        out_shape=shapes,
        in_specs=[hbm] * 10,
        out_specs=(hbm,) * 5,
        scratch_shapes=[
            *[pltpu.VMEM((channels, length), bf16)] * 4,
            pltpu.VMEM((feat, channels), f32),
            rows(owners, 4),
            rows(reducers, 4),
            *[pltpu.VMEM((channels, length), bf16)] * 4,
            pltpu.VMEM(filter_weight.shape, f32),
            *[pltpu.VMEM(table.shape, f32) for table in tables],
            pltpu.VMEM((2, tables[0].shape[1], 3 * tables[0].shape[2]), bf16),
            pltpu.VMEM((4, *tables[1].shape[1:]), bf16),
            pltpu.VMEM((4, *tables[2].shape[1:]), bf16),
            rows(2 * groups, per),
            pltpu.VMEM((feat, 2 * LANES), f32),
            rows(owners, 4),
            rows(shards, 4),
            rows(owners, 4),
            rows(owners, 4),
            rows(owners, 4),
            rows(owners, 4),
            rows(reducers, 4),
            rows(owners, 4),
            rows(shards, 4),
            rows(shards, 4),
            pltpu.SemaphoreType.DMA((5,)),
            pltpu.SemaphoreType.DMA((5,)),
            pltpu.SemaphoreType.DMA((4,)),
            pltpu.SemaphoreType.DMA,
            pltpu.SemaphoreType.DMA((2, groups)),
            pltpu.SemaphoreType.DMA((2, groups)),
            pltpu.SemaphoreType.DMA((7,)),
            pltpu.SemaphoreType.DMA((7,)),
            pltpu.SemaphoreType.REGULAR,
            pltpu.SemaphoreType.REGULAR,
            pltpu.SemaphoreType.REGULAR,
        ],
        compiler_params=pltpu.CompilerParams(
            collective_id=0, has_side_effects=True, vmem_limit_bytes=56 * 1024 * 1024
        ),
    )(gate_input, key_input, value_input, features, filter_weight, out_grad, *tables)
    return pl.pallas_call(
        hand_over,
        out_shape=shapes,
        in_specs=[hbm] * 5,
        out_specs=(hbm,) * 5,
        scratch_shapes=[
            *[pltpu.VMEM((channels, length), bf16)] * 4,
            pltpu.VMEM((feat, channels), f32),
            pltpu.SemaphoreType.DMA((5,)),
            pltpu.SemaphoreType.DMA((5,)),
        ],
        compiler_params=pltpu.CompilerParams(vmem_limit_bytes=56 * 1024 * 1024),
    )(*results)


def solution(mesh):
    placed = (
        P("ch", "ctx"),
        P("ch", "ctx"),
        P("ch", "ctx"),
        P("ch", "ctx"),
        P(None, "ch"),
        P("ch", "ctx"),
    )
    return jax.shard_map(
        on_device,
        mesh=mesh,
        in_specs=placed,
        out_specs=(P("ch", "ctx"), P("ch", "ctx"), P("ch", "ctx"), P("ch", "ctx"), P(None, "ch")),
        check_vma=False,
    )
```

```python
import functools
import math

import jax
import jax.numpy as jnp
import numpy as np
from jax import lax
from jax.experimental import pallas as pl
from jax.experimental.pallas import tpu as pltpu
from jax.sharding import PartitionSpec as P

MESH = pl.DeviceIdType.MESH
HIGHEST = lax.Precision.HIGHEST
f32 = jnp.float32
bf16 = jnp.bfloat16
LANES = 128


def make_tables(shards):
    outer = 2 * shards
    padded = outer * LANES
    rows = -(-(shards + 1) // 8) * 8
    r = np.arange(rows)
    live = (r <= shards).astype(np.float64)
    natural = np.arange(shards)
    by_parity = np.concatenate([natural[0::2], natural[1::2]])

    def angles(left, right, period):
        return 2.0 * np.pi * ((left[:, None] * right[None, :]) % period) / period

    first, last = [], []
    weight = np.where((r == 0) | (r == shards), 1.0, 2.0) * live / padded
    for order in (natural, by_parity):
        turn = angles(r, order, outer)
        table = np.concatenate([np.cos(turn), np.sin(turn)], axis=0) * np.tile(live, 2)[:, None]
        first.append(table)
        turn = angles(order, r, outer)
        table = np.concatenate([np.cos(turn) * weight, -np.sin(turn) * weight], axis=1)
        last.append(table)
    q = np.arange(LANES)
    turn = angles(q, q, LANES)
    cos, sin = np.cos(turn), np.sin(turn)
    forward = np.block([[cos, -sin], [sin, cos]])
    backward = np.block([[cos, sin], [-sin, cos]])
    turn = angles(r, q, padded)
    twist = [np.cos(turn), np.sin(turn)]
    return tuple(np.stack(table).astype(np.float32) for table in (first, last, [forward, backward], twist))


def halves(x):
    high = x.astype(bf16)
    return high, (x - high.astype(f32)).astype(bf16)


def dot(a, b):
    return jnp.dot(a, b, preferred_element_type=f32)


def rows_by_rows(a, b):
    return lax.dot_general(a, b, (((1,), (1,)), ((), ())), preferred_element_type=f32)


def dot_t(a, b):
    return lax.dot_general(a, b, (((1,), (1,)), ((), ())), precision=HIGHEST, preferred_element_type=f32)


def spectra(signals, first, mid, cos, sin):
    rows = cos.shape[0]
    high, low = halves(jnp.concatenate(signals, axis=1))
    outer = dot(first, jnp.concatenate([high, low, high], axis=0))
    turned = []
    for index in range(len(signals)):
        part = outer[:, index * LANES : (index + 1) * LANES]
        along, across = part[:rows], part[rows:]
        turned.append(
            jnp.concatenate([along * cos - across * sin, -(across * cos + along * sin)], axis=1)
        )
    high, low = halves(jnp.concatenate(turned, axis=0))
    return dot(jnp.concatenate([high, low, high], axis=1), mid[...])


def signals_of(products, last, mid, cos, sin):
    rows = cos.shape[0]
    high, low = halves(jnp.concatenate(products, axis=0))
    inner = dot(jnp.concatenate([high, low, high], axis=1), mid[...])
    turned = []
    for index in range(len(products)):
        part = inner[index * rows : (index + 1) * rows]
        real, imag = part[:, :LANES], part[:, LANES:]
        turned.append(jnp.concatenate([real * cos - imag * sin, imag * cos + real * sin], axis=0))
    high, low = halves(jnp.concatenate(turned, axis=1))
    return dot(last[0], high) + dot(last[0], low) + dot(last[1], high)


def times(a, b):
    ar, ai, br, bi = a[:, :LANES], a[:, LANES:], b[:, :LANES], b[:, LANES:]
    return jnp.concatenate([ar * br - ai * bi, ar * bi + ai * br], axis=1)


def times_conj(a, b):
    ar, ai, br, bi = a[:, :LANES], a[:, LANES:], b[:, :LANES], b[:, LANES:]
    return jnp.concatenate([ar * br + ai * bi, ai * br - ar * bi], axis=1)


def kernel(
    shards,
    groups,
    gate_in,
    key_in,
    value_in,
    feats_in,
    weight_in,
    upstream_in,
    first_in,
    last_in,
    mid_in,
    twist_in,
    output_hbm,
    gate_grad_hbm,
    key_grad_hbm,
    value_grad_hbm,
    weight_grad_hbm,
    output,
    gate_grad,
    key_grad,
    value_grad,
    weight_grad,
    recv_out,
    recv_sum,
    gate,
    key,
    value,
    upstream,
    weight,
    first,
    last,
    mid,
    twist,
    first_split,
    last_split,
    mid_split,
    feats,
    feats_all,
    send_sig,
    recv_sig,
    send_filt,
    recv_filt,
    send_taps,
    recv_taps,
    send_part,
    recv_part,
    send_sum,
    send_out,
    in_sems,
    out_sems,
    table_sems,
    own_sem,
    feat_sems,
    feat_sent,
    send_sems,
    recv_sems,
    hello,
    ready,
    all_in,
):
    me = lax.axis_index("ctx")
    group = lax.axis_index("ch")
    owners = shards // 2
    chip = me // 2
    core = me % 2
    scaling = 1.0 / math.sqrt(shards * LANES)
    deep = 4 if groups % 4 == 0 else 1
    wide = groups // deep
    rank = (group % deep) * wide + group // deep
    kind = jnp.minimum(group % deep, 2)
    known = wide * jnp.minimum(kind + 1, 2)
    settled = min(2 * wide, groups)
    greeters = known - jnp.where(kind < 2, 1, 0)
    hub = 1
    at_hub = chip == hub
    reducers = owners // 4
    ring = owners // 4
    along = chip // 4
    nearness = jnp.where(
        along < 2, along, jnp.where(along == ring - 1, 2, jnp.where(along == 2, 3, reducers))
    )
    my_reducer = nearness * 2 + chip % 4
    reducer = jnp.logical_and(core == 1, jnp.logical_and(chip % 4 < 2, my_reducer < reducers))

    def reducer_chip(k):
        near = k // 2
        return jnp.where(near == 2, ring - 1, jnp.where(near == 3, 2, near)) * 4 + k % 2

    def ranked(r):
        return (r % wide) * deep + r // wide

    inputs = [
        pltpu.make_async_copy(src, dst, in_sems.at[n])
        for n, (src, dst) in enumerate(
            [(key_in, key), (value_in, value), (upstream_in, upstream), (gate_in, gate), (weight_in, weight)]
        )
    ]
    tables = [
        pltpu.make_async_copy(src, dst, table_sems.at[n])
        for n, (src, dst) in enumerate([(first_in, first), (mid_in, mid), (twist_in, twist), (last_in, last)])
    ]

    def push(src, dst, phase, where):
        pltpu.make_async_remote_copy(
            src_ref=src,
            dst_ref=dst,
            send_sem=send_sems.at[phase],
            recv_sem=recv_sems.at[phase],
            device_id=where,
            device_id_type=MESH,
        ).start()

    def tell(semaphore, where):
        pl.semaphore_signal(semaphore, inc=1, device_id=where, device_id_type=MESH)

    def loop(low, high, step):
        def body(k, carry):
            step(k)
            return carry

        lax.fori_loop(low, high, body, 0)

    def far_first(low, count, step):
        loop(count // 2, count, step)
        loop(low, count // 2, step)

    def others(low, high, step):
        def guarded(r):
            @pl.when(r != rank)
            def _():
                step(ranked(r))

        loop(low, high, guarded)

    def arrived(ref, count, phase):
        part = ref.at[pl.ds(0, count)]
        pltpu.make_async_copy(part, part, recv_sems.at[phase]).wait()

    def sent(ref, count, phase):
        part = ref.at[pl.ds(0, count)]
        pltpu.make_async_copy(part, part, send_sems.at[phase]).wait()

    for copy in inputs:
        copy.start()

    barrier = pltpu.get_barrier_semaphore()
    neighbour = {"ctx": me ^ 1, "ch": group}
    even_feats, odd_feats = feats.at[group], feats.at[groups + group]
    own_feats = pltpu.make_async_copy(feats_in, odd_feats, own_sem)

    def push_feats(src, which, other):
        pltpu.make_async_remote_copy(
            src_ref=src,
            dst_ref=feats.at[which * groups + group],
            send_sem=feat_sent.at[which, other],
            recv_sem=feat_sems.at[which, group],
            device_id={"ctx": 2 * chip + 1, "ch": other},
            device_id_type=MESH,
        ).start()

    def await_block(sems, which, other):
        part = feats.at[which * groups + other]
        pltpu.make_async_copy(part, part, sems.at[which, other]).wait()

    def await_feats(other):
        await_block(feat_sems, 0, other)
        await_block(feat_sems, 1, other)

    @pl.when(core == 1)
    def _():
        tell(barrier, neighbour)

        @pl.when(jnp.logical_not(at_hub))
        def _():
            tell(barrier, {"ctx": 2 * hub, "ch": group})

        def greet(other):
            tell(barrier, {"ctx": me, "ch": other})

            @pl.when(jnp.logical_not(at_hub))
            def _():
                tell(barrier, {"ctx": me - 1, "ch": other})

        others(jnp.where(kind < 2, wide * kind, groups), groups, greet)
        pl.semaphore_wait(barrier, greeters + jnp.where(at_hub, 1, 0))
        others(0, known, lambda other: push_feats(feats_in, 1, other))
        own_feats.start()
        for copy in tables:
            copy.start()

        @pl.when(at_hub)
        def _():
            tell(hello, neighbour)
            await_block(feat_sems, 0, group)
            others(0, known, lambda other: push_feats(even_feats, 0, other))

    @pl.when(jnp.logical_and(core == 0, at_hub))
    def _():
        tell(barrier, neighbour)
        pl.semaphore_wait(hello, 1)
        push_feats(feats_in, 0, group)

        pl.semaphore_wait(barrier, owners)
        loop(0, owners, lambda k: tell(ready, {"ctx": 2 * k + 1, "ch": group}))

    @pl.when(jnp.logical_and(core == 0, jnp.logical_not(at_hub)))
    def _():
        pl.semaphore_wait(barrier, greeters + 1)

        @pl.when(jnp.logical_not(at_hub))
        def _():
            tell(hello, neighbour)

        others(0, known, lambda other: push_feats(feats_in, 0, other))
        push_feats(feats_in, 0, group)

    for copy in inputs[:4]:
        copy.wait()
    key_vals, value_vals = key[...].astype(f32), value[...].astype(f32)
    gate_vals, up_vals = gate[...].astype(f32), upstream[...].astype(f32)
    mixed, inner = key_vals * value_vals, up_vals * gate_vals
    send_sig[:, 0, :] = mixed[:owners]
    send_sig[:, 1, :] = mixed[owners:]
    send_sig[:, 2, :] = inner[:owners]
    send_sig[:, 3, :] = inner[owners:]

    def push_sig(k):
        to = chip ^ k
        push(send_sig.at[to], recv_sig.at[me], 1, {"ctx": 2 * to + 1, "ch": group})

    @pl.when(core == 0)
    def _():
        @pl.when(jnp.logical_not(at_hub))
        def _():
            pl.semaphore_wait(ready, 1)

        far_first(0, owners, push_sig)

    inputs[4].wait()

    @pl.when(core == 1)
    def _():
        recv_sig[pl.ds(me, 1)] = send_sig[pl.ds(chip, 1)]
        pl.semaphore_wait(ready, 1)

        far_first(1, owners, push_sig)

        @pl.when(jnp.logical_not(at_hub))
        def _():
            pl.semaphore_wait(hello, 1)
            tell(ready, neighbour)

        eye = (
            lax.broadcasted_iota(jnp.int32, (2 * owners, 2 * owners), 0)
            == lax.broadcasted_iota(jnp.int32, (2 * owners, 2 * owners), 1)
        ).astype(f32)
        high, low = halves(dot_t(eye, weight[...]) * scaling)
        weight_t = jnp.concatenate([high, high, low], axis=1)
        for copy in tables:
            copy.wait()
        cos, sin = twist[0], twist[1]
        rows = cos.shape[0]
        for n in range(2):
            high, low = halves(first[n])
            first_split[n] = jnp.concatenate([high, high, low], axis=1)
            last_split[2 * n], last_split[2 * n + 1] = halves(last[n])
            high, low = halves(mid[n])
            mid_split[n] = jnp.concatenate([high, high, low], axis=0)
        forward, backward = mid_split.at[0], mid_split.at[1]
        lasts = [(last_split[0], last_split[1]), (last_split[2], last_split[3])]

        own_feats.wait()

        @pl.when(jnp.logical_not(at_hub))
        def _():
            await_block(feat_sems, 0, group)

        def push_both(other):
            push_feats(even_feats, 0, other)
            push_feats(odd_feats, 1, other)

        @pl.when(kind == 2)
        def _():
            pl.semaphore_wait(all_in, 1)
            others(known, groups, push_both)

        def trade(other):
            await_feats(other)
            push_both(other)

        def push_filt(k):
            to = chip ^ k
            push(send_filt.at[to], recv_filt.at[chip], 2, {"ctx": 2 * to + 1, "ch": group})

        def filter_phase():
            @pl.when(kind == 0)
            def _():
                others(3 * wide, groups, trade)
                others(2 * wide, min(3 * wide, groups), await_feats)

                @pl.when(2 * wide < groups)
                def _():
                    for step in range(2, deep):
                        tell(all_in, {"ctx": me, "ch": group + step})

            @pl.when(kind == 1)
            def _():
                others(0, settled, await_feats)
                others(settled, groups, trade)

            @pl.when(kind == 2)
            def _():
                others(0, groups, await_feats)

            per = feats.shape[1]
            feats_all[...] = jnp.concatenate(
                [
                    feats[:groups].reshape(groups * per, LANES),
                    feats[groups:].reshape(groups * per, LANES),
                ],
                axis=1,
            )
            high, low = halves(feats_all[...])
            filt = dot(weight_t, jnp.concatenate([high, low, high], axis=0))
            send_filt[:, 0, :] = filt[:owners, :LANES]
            send_filt[:, 1, :] = filt[:owners, LANES:]
            send_filt[:, 2, :] = filt[owners:, :LANES]
            send_filt[:, 3, :] = filt[owners:, LANES:]
            far_first(1, owners, push_filt)
            recv_filt[pl.ds(chip, 1)] = send_filt[pl.ds(chip, 1)]

            @pl.when(kind == 0)
            def _():
                others(2 * wide, min(3 * wide, groups), push_both)

        @pl.when(kind == 0)
        def _():
            others(0, wide, await_feats)
            others(wide, jnp.minimum(2 * wide, groups), trade)

        arrived(recv_sig, shards - 1, 1)
        specs = spectra([recv_sig[:, n, :] for n in range(4)], first_split[0], forward, cos, sin)
        mixed_specs = [specs[:rows], specs[rows : 2 * rows]]
        inner_specs = [specs[2 * rows : 3 * rows], specs[3 * rows :]]
        taps = signals_of(
            [times_conj(inner_specs[n], mixed_specs[n]) for n in range(2)], lasts[1], backward, cos, sin
        )
        send_taps[:, 0, :] = taps[:owners, :LANES]
        send_taps[:, 1, :] = taps[owners:, :LANES]
        send_taps[:, 2, :] = taps[:owners, LANES:]
        send_taps[:, 3, :] = taps[owners:, LANES:]

        def push_taps(k):
            to = chip ^ k
            push(send_taps.at[to], recv_taps.at[chip], 3, {"ctx": 2 * to + 1, "ch": group})

        far_first(1, owners, push_taps)
        recv_taps[pl.ds(chip, 1)] = send_taps[pl.ds(chip, 1)]

        filter_phase()

        arrived(recv_taps, owners - 1, 3)
        taps_here = jnp.concatenate(
            [
                jnp.concatenate([recv_taps[:, 0, :], recv_taps[:, 1, :]], axis=1),
                jnp.concatenate([recv_taps[:, 2, :], recv_taps[:, 3, :]], axis=1),
            ],
            axis=0,
        )
        feats_high, feats_low = halves(feats_all[...])
        high, low = halves(taps_here)
        part = rows_by_rows(high, feats_high) + rows_by_rows(low, feats_high) + rows_by_rows(high, feats_low)
        pairs = jnp.concatenate([part[:owners], part[owners:]], axis=1)
        for n in range(4):
            send_part[:, n, :] = pairs[n * reducers : (n + 1) * reducers]

        def push_part(k):
            @pl.when(jnp.logical_not(jnp.logical_and(reducer, k == my_reducer)))
            def _():
                push(send_part.at[k], recv_part.at[chip], 5, {"ctx": 2 * reducer_chip(k) + 1, "ch": group})

        loop(0, reducers, push_part)

        @pl.when(reducer)
        def _():
            recv_part[pl.ds(chip, 1)] = send_part[pl.ds(my_reducer, 1)]

        arrived(recv_filt, owners - 1, 2)
        filt_specs = spectra(
            [
                jnp.concatenate([recv_filt[:, 2 * n, :], recv_filt[:, 2 * n + 1, :]], axis=0)
                for n in range(2)
            ],
            first_split[1],
            forward,
            cos,
            sin,
        )
        filt_specs = [filt_specs[:rows], filt_specs[rows:]]
        results = signals_of(
            [times(mixed_specs[n], filt_specs[n]) for n in range(2)]
            + [times_conj(inner_specs[n], filt_specs[n]) for n in range(2)],
            lasts[0],
            backward,
            cos,
            sin,
        )
        for n in range(4):
            send_out[:, n, :] = results[:, n * LANES : (n + 1) * LANES]

        def push_out(k):
            to = me ^ k
            push(send_out.at[to], recv_out.at[chip], 4, {"ctx": to, "ch": group})

        far_first(1, shards, push_out)
        recv_out[pl.ds(chip, 1)] = send_out[pl.ds(me, 1)]

        @pl.when(reducer)
        def _():
            arrived(recv_part, owners - 1, 5)
            send_sum[pl.ds(0, 1)] = jnp.sum(recv_part[...], axis=0, keepdims=True) * (scaling * scaling)

            def push_sum(k):
                push(send_sum.at[0], recv_sum.at[my_reducer], 6, {"ctx": me ^ k, "ch": group})

            far_first(1, shards, push_sum)
            recv_sum[pl.ds(my_reducer, 1)] = send_sum[pl.ds(0, 1)]
            sent(send_part, reducers - 1, 5)

        @pl.when(jnp.logical_not(reducer))
        def _():
            sent(send_part, reducers, 5)

        def sent_odd(other):
            await_block(feat_sent, 1, other)

        others(0, groups, sent_odd)
        others(jnp.where(at_hub, 0, known), groups, lambda other: await_block(feat_sent, 0, other))
        sent(send_filt, owners - 1, 2)
        sent(send_taps, owners - 1, 3)
        sent(send_sig, owners - 1, 1)
        arrived(recv_out, owners - 1, 4)
        sent(send_out, shards - 1, 4)

    @pl.when(core == 0)
    def _():
        await_block(feat_sent, 0, group)

        @pl.when(jnp.logical_not(at_hub))
        def _():
            others(0, known, lambda other: await_block(feat_sent, 0, other))

        sent(send_sig, owners, 1)
        arrived(recv_out, owners, 4)

    results = [
        pltpu.make_async_copy(ref, target, out_sems.at[n])
        for n, (ref, target) in enumerate(
            [
                (output, output_hbm),
                (gate_grad, gate_grad_hbm),
                (key_grad, key_grad_hbm),
                (value_grad, value_grad_hbm),
                (weight_grad, weight_grad_hbm),
            ]
        )
    ]
    conv = jnp.concatenate([recv_out[:, 0, :], recv_out[:, 1, :]], axis=0)
    output[...] = (gate[...].astype(f32) * conv).astype(bf16)
    results[0].start()
    gate_grad[...] = (upstream[...].astype(f32) * conv).astype(bf16)
    results[1].start()
    mixed_grad = jnp.concatenate([recv_out[:, 2, :], recv_out[:, 3, :]], axis=0)
    key_grad[...] = (mixed_grad * value[...].astype(f32)).astype(bf16)
    results[2].start()
    value_grad[...] = (mixed_grad * key[...].astype(f32)).astype(bf16)
    results[3].start()

    @pl.when(reducer)
    def _():
        arrived(recv_sum, reducers - 1, 6)

    @pl.when(jnp.logical_not(reducer))
    def _():
        arrived(recv_sum, reducers, 6)

    sums = jnp.concatenate([recv_sum[:, n, :] for n in range(4)], axis=0)
    half = sums.shape[1] // 2
    eye = (
        lax.broadcasted_iota(jnp.int32, (half, half), 0) == lax.broadcasted_iota(jnp.int32, (half, half), 1)
    ).astype(bf16)
    high, low = halves(jnp.concatenate([sums[:, :half], sums[:, half:]], axis=0))
    weight_grad[...] = rows_by_rows(eye, high) + rows_by_rows(eye, low)
    results[4].start()

    @pl.when(reducer)
    def _():
        sent(send_sum, shards - 1, 6)

    for copy in results:
        copy.wait()


def hand_over(*refs):
    sources, targets, held = refs[:5], refs[5:10], refs[10:15]
    in_sems, out_sems = refs[15:]
    loads = [pltpu.make_async_copy(source, ref, in_sems.at[n]) for n, (source, ref) in enumerate(zip(sources, held))]
    stores = [pltpu.make_async_copy(ref, target, out_sems.at[n]) for n, (ref, target) in enumerate(zip(held, targets))]
    for load in loads:
        load.start()
    for load, store in zip(loads, stores):
        load.wait()
        store.start()
    for store in stores:
        store.wait()


def on_device(gate_input, key_input, value_input, features, filter_weight, out_grad):
    shards, groups = lax.axis_size("ctx"), lax.axis_size("ch")
    channels, length = gate_input.shape
    feat = filter_weight.shape[0]
    owners = shards // 2
    reducers = owners // 4
    assert channels == 2 * owners and length == LANES and feat == LANES // 2
    tables = make_tables(shards)
    hbm = pl.BlockSpec(memory_space=pl.ANY)
    rows = lambda count, width: pltpu.VMEM((count, width, LANES), f32)
    block = jax.ShapeDtypeStruct((channels, length), bf16)
    per = features.shape[0]
    shapes = (block, block, block, block, jax.ShapeDtypeStruct((feat, channels), f32))
    results = pl.pallas_call(
        functools.partial(kernel, shards, groups),
        out_shape=shapes,
        in_specs=[hbm] * 10,
        out_specs=(hbm,) * 5,
        scratch_shapes=[
            *[pltpu.VMEM((channels, length), bf16)] * 4,
            pltpu.VMEM((feat, channels), f32),
            rows(owners, 4),
            rows(reducers, 4),
            *[pltpu.VMEM((channels, length), bf16)] * 4,
            pltpu.VMEM(filter_weight.shape, f32),
            *[pltpu.VMEM(table.shape, f32) for table in tables],
            pltpu.VMEM((2, tables[0].shape[1], 3 * tables[0].shape[2]), bf16),
            pltpu.VMEM((4, *tables[1].shape[1:]), bf16),
            pltpu.VMEM((2, 3 * tables[2].shape[1], tables[2].shape[2]), bf16),
            rows(2 * groups, per),
            pltpu.VMEM((feat, 2 * LANES), f32),
            rows(owners, 4),
            rows(shards, 4),
            rows(owners, 4),
            rows(owners, 4),
            rows(owners, 4),
            rows(owners, 4),
            rows(reducers, 4),
            rows(owners, 4),
            rows(shards, 4),
            rows(shards, 4),
            pltpu.SemaphoreType.DMA((5,)),
            pltpu.SemaphoreType.DMA((5,)),
            pltpu.SemaphoreType.DMA((4,)),
            pltpu.SemaphoreType.DMA,
            pltpu.SemaphoreType.DMA((2, groups)),
            pltpu.SemaphoreType.DMA((2, groups)),
            pltpu.SemaphoreType.DMA((7,)),
            pltpu.SemaphoreType.DMA((7,)),
            pltpu.SemaphoreType.REGULAR,
            pltpu.SemaphoreType.REGULAR,
            pltpu.SemaphoreType.REGULAR,
        ],
        compiler_params=pltpu.CompilerParams(
            collective_id=0, has_side_effects=True, vmem_limit_bytes=56 * 1024 * 1024
        ),
    )(gate_input, key_input, value_input, features, filter_weight, out_grad, *tables)
    return pl.pallas_call(
        hand_over,
        out_shape=shapes,
        in_specs=[hbm] * 5,
        out_specs=(hbm,) * 5,
        scratch_shapes=[
            *[pltpu.VMEM((channels, length), bf16)] * 4,
            pltpu.VMEM((feat, channels), f32),
            pltpu.SemaphoreType.DMA((5,)),
            pltpu.SemaphoreType.DMA((5,)),
        ],
        compiler_params=pltpu.CompilerParams(vmem_limit_bytes=56 * 1024 * 1024),
    )(*results)


def solution(mesh):
    placed = (
        P("ch", "ctx"),
        P("ch", "ctx"),
        P("ch", "ctx"),
        P("ch", "ctx"),
        P(None, "ch"),
        P("ch", "ctx"),
    )
    return jax.shard_map(
        on_device,
        mesh=mesh,
        in_specs=placed,
        out_specs=(P("ch", "ctx"), P("ch", "ctx"), P("ch", "ctx"), P("ch", "ctx"), P(None, "ch")),
        check_vma=False,
    )
```
